128 devices in a mesh: gx: 8 (over z, core), gy: 16 (over y, x).
Axes of the slice: x: 4, y: 4, z: 4, core: 2. Of those that a mesh axis runs over, the one named last changes fastest.
Arguments:
- dyn_state: bfloat16 [40, 64, 65536], P(None, None, ('gx', 'gy')), may hold values from -6 to 6
- span_map: int32 [65536], P(('gx', 'gy')), may hold values from 0 to 65535, as said below
- sunlit: int32 [65536], P(('gx', 'gy')), may hold values from 0 to 1, as said below
- coszen: float32 [65536], P(('gx', 'gy')), may hold values from 0.05 to 1
- albedo: float32 [65536], P(('gx', 'gy')), may hold values from 0.05 to 0.9
- ground_temp: float32 [65536], P(('gx', 'gy')), may hold values from -6 to 6
- aerosol: bfloat16 [58, 64, 65536], P(None, None, ('gx', 'gy')), may hold values from -6 to 6
- k_long: bfloat16 [128, 98], replicated, may hold values from -1 to 1
- planck: float32 [128], replicated, may hold values from 0.25 to 0.5
- k_short: bfloat16 [112, 98], replicated, may hold values from -0.625 to 0.625
- solar_flux: float32 [112], replicated, may hold values from 2 to 8
Outputs:
- heating: float32 [64, 65536], P(None, ('gx', 'gy'))
- surface: float32 [2, 65536], P(None, ('gx', 'gy'))
The draws below stay inside these ranges and needn't reach their ends.
Inputs may be any that keep to these rules, and one draw needn't show every extreme that they name: span_map is a permutation of 0 .. 65535. Of the 512 columns of a device, exactly 64 have span positions on the same device (position // 512 equal to the device's index along gx+gy); to every other device it sends either 4 or 3 columns, and 4 to some. At most 448 of a device's 512 span-order columns are sunlit, and some device has exactly 448. Two devices at the same gy index whose gx indices differ by half of gx's size hold together at most 512 sunlit columns.
All inputs are finite; a program needn't handle non-finite values.
Results may differ from the reference program's by a relative error of at most 0.0005.
Values may be sent and summed in bfloat16 or wider, within the bound.
No kernel may reach another device: no remote copies, remote signals or barrier semaphores. Data moves between devices by JAX's collectives and lax.ppermute only.
A program may use at most 128 MiB of HBM per device.

```python
import math
import jax
import jax.numpy as jnp
from jax import lax

COL_DEV = 512
LEV = 64
NFIELD = 40
NAER = 58
GLW = 128
GSW = 112
KEEP = 64
SUN_MAX = 448
NCOL = 65536
N_GX = 8
N_GY = 16


def draw_span_map(key, part):
    key = jax.random.fold_in(key, 7)
    devices = N_GX * N_GY
    key_labels, key_roles, key_slots = jax.random.split(key, 3)
    labels = jax.random.permutation(key_labels, devices).astype(jnp.int32)
    inverse = jnp.zeros((devices,), jnp.int32).at[labels].set(jnp.arange(devices, dtype=jnp.int32))
    roles = jax.vmap(lambda subkey: jax.random.permutation(subkey, COL_DEV))(jax.random.split(key_roles, devices)).astype(jnp.int32)
    arrival_slots = jax.vmap(lambda subkey: jax.random.permutation(subkey, COL_DEV))(jax.random.split(key_slots, devices)).astype(jnp.int32)
    device_ids = jnp.arange(devices, dtype=jnp.int32)[:, None]
    shifted = (labels[device_ids] + 1 + jnp.maximum(roles - KEEP, 0) % (devices - 1)) % devices
    target = jnp.where(roles < KEEP, device_ids, inverse[shifted])
    slot_index = arrival_slots[target, roles]
    return (target * COL_DEV + slot_index).reshape(-1).astype(jnp.int32)


def draw_sunlit(key, part):
    key = jax.random.fold_in(key, 11)
    devices = N_GX * N_GY
    half_devices = devices // 2
    key_first, key_forced, key_extra, key_flip, key_order = jax.random.split(key, 5)
    first = jax.random.randint(key_first, (half_devices,), COL_DEV // 8, SUN_MAX + 1)
    forced = jax.random.randint(key_forced, (), 0, half_devices)
    first = jnp.where(jnp.arange(half_devices) == forced, SUN_MAX, first)
    extra = jax.random.randint(key_extra, (half_devices,), 0, COL_DEV // 8 + 1)
    second = COL_DEV - first - extra
    flipped = jax.random.randint(key_flip, (half_devices,), 0, 2)
    lower = jnp.where(flipped == 1, first, second)
    upper = jnp.where(flipped == 1, second, first)
    counts = jnp.concatenate([lower, upper]).astype(jnp.int32)
    ranking = jax.vmap(lambda subkey: jax.random.permutation(subkey, COL_DEV))(jax.random.split(key_order, devices)).astype(jnp.int32)
    return (ranking < counts[:, None]).astype(jnp.int32).reshape(-1)


def draw_coszen(key, part):
    key = jax.random.fold_in(key, 19)
    values = jnp.exp(jax.random.uniform(key, (NCOL,), jnp.float32, math.log(0.05), 0.0))
    return jnp.clip(values, 0.05, 1.0).astype(jnp.float32)


def draw_albedo(key, part):
    key = jax.random.fold_in(key, 23)
    key_dark = jax.random.fold_in(key, 1)
    values = jax.random.uniform(key_dark, (NCOL,), jnp.float32, 0.05, 0.9)
    return values.astype(jnp.float32)


def draw_aerosol(key, part):
    key = jax.random.fold_in(key, 13)
    values = jax.random.truncated_normal(key, -6.0, 6.0, (NAER, LEV, NCOL), jnp.float32)
    return values.astype(jnp.bfloat16)


def draw_k_long(key, part):
    key = jax.random.fold_in(key, 17)
    key_base = jax.random.fold_in(key, 0)
    width = NFIELD + NAER
    base = jax.random.truncated_normal(key_base, -6.0, 6.0, (GLW, width), jnp.float32) * (1.0 / math.sqrt(width))
    return base.astype(jnp.bfloat16)


def block_levels(stream_key, dims, cuts, smallest, top_value):
    gain = 1.0
    for dim, parts in cuts:
        draws = jax.random.uniform(jax.random.fold_in(jax.random.fold_in(stream_key, 6), dim), (parts,), jnp.float32, smallest / len(cuts), top_value / len(cuts))
        gain = gain * jnp.repeat(jnp.exp(draws), dims[dim] // parts).reshape((-1,) + (1,) * (len(dims) - 1 - dim))
    return gain


def bell_draw(key, extent, deviation, limit, cuts=(), kind=jnp.bfloat16):
    entries = deviation * jax.random.normal(key, extent, jnp.float32)
    if cuts:
        entries = entries * block_levels(key, extent, cuts, -0.22, 0.18)
    return jnp.clip(entries, -limit, limit).astype(kind)


def setup_inputs(seed: int = 0) -> dict:
    key_list = jax.random.split(jax.random.key(seed), 12)
    return {
        "dyn_state": bell_draw(key_list[0], (NFIELD, LEV, NCOL), 1.0, 6.0, ((2, 128),)),
        "span_map": draw_span_map(jax.random.fold_in(key_list[11], 71), 0),
        "sunlit": draw_sunlit(jax.random.fold_in(key_list[11], 71), 0),
        "coszen": draw_coszen(jax.random.fold_in(key_list[11], 71), 0),
        "albedo": draw_albedo(jax.random.fold_in(key_list[11], 71), 0),
        "ground_temp": bell_draw(key_list[5], (NCOL,), 1.0, 6.0, ((0, 128),), jnp.float32),
        "aerosol": draw_aerosol(jax.random.fold_in(key_list[11], 71), 0),
        "k_long": draw_k_long(jax.random.fold_in(key_list[11], 71), 0),
        "planck": jnp.clip(jnp.exp(jax.random.uniform(key_list[8], (GLW,), jnp.float32, math.log(0.25), math.log(0.5))), 0.25, 0.5),
        "k_short": bell_draw(key_list[9], (GSW, NFIELD + NAER), (NFIELD + NAER) ** -0.5, 0.625),
        "solar_flux": jnp.clip(jnp.exp(jax.random.uniform(key_list[10], (GSW,), jnp.float32, math.log(2.0), math.log(8.0))), 2.0, 8.0),
    }


DIFFUSE = 1.66
SCATTER = 0.3
SW_DEPTH = 2.0


def longwave(fields, k_long, planck, ground_temp):
    gpoints = k_long.shape[0]
    block_size = math.gcd(gpoints, 32)
    warmth = jax.nn.softplus(fields[0].astype(jnp.float32))
    surface_emit = jax.nn.softplus(ground_temp)
    fields_wide = fields.astype(jnp.float32)

    def one_block(pieces):
        absorb, planck_part = pieces
        optical = jax.nn.softplus(jnp.einsum("gk,klc->lgc", absorb.astype(jnp.float32), fields_wide))
        transmit = jnp.exp(-DIFFUSE * optical)
        emitted = (1.0 - transmit) * planck_part[None, :, None] * warmth[:, None, :]

        def downward(carried, slices):
            return slices[0] * carried + slices[1], jnp.sum(carried, axis=0)

        floor_down, down_sum = lax.scan(downward, jnp.zeros(transmit.shape[1:], jnp.float32), (transmit, emitted))
        surface_up = planck_part[:, None] * surface_emit[None, :]

        def upward(carried, slices):
            upper = slices[0] * carried + slices[1]
            return upper, jnp.sum(upper, axis=0)

        _, up_sum = lax.scan(upward, surface_up, (transmit, emitted), reverse=True)
        floor_sum = jnp.sum(floor_down, axis=0)
        balance = jnp.concatenate([down_sum - up_sum, (floor_sum - jnp.sum(surface_up, axis=0))[None]], axis=0)
        return balance[:-1] - balance[1:], floor_sum

    heating_parts, floor_parts = lax.map(one_block, (k_long.reshape(-1, block_size, k_long.shape[1]), planck.reshape(-1, block_size)))
    return jnp.sum(heating_parts, axis=0) / gpoints, jnp.sum(floor_parts, axis=0) / gpoints


def shortwave(fields, k_short, solar_flux, cosine, albedo):
    gpoints = k_short.shape[0]
    block_size = math.gcd(gpoints, 32)
    fields_wide = fields.astype(jnp.float32)
    depth_scale = SW_DEPTH / fields.shape[1]

    def one_block(pieces):
        absorb, solar_part = pieces
        optical = depth_scale * jax.nn.softplus(jnp.einsum("gk,klc->lgc", absorb.astype(jnp.float32), fields_wide))
        direct = jnp.exp(-optical / cosine[None, None, :])
        diffuse = jnp.exp(-DIFFUSE * optical)
        beam_top = solar_part[:, None] * cosine[None, :]

        def downward(carried, slices):
            beam_flux, spread = carried
            direct_t, diffuse_t = slices
            scatter = SCATTER * (1.0 - direct_t) * beam_flux
            return (direct_t * beam_flux, diffuse_t * spread + scatter), (jnp.sum(beam_flux + spread, axis=0), scatter)

        start_pair = (beam_top, jnp.zeros(beam_top.shape, jnp.float32))
        (beam_floor, spread_floor), (down_sum, scattered) = lax.scan(downward, start_pair, (direct, diffuse))
        reflect_up = albedo[None, :] * (beam_floor + spread_floor)

        def upward(carried, slices):
            upper = slices[0] * carried + slices[1]
            return upper, jnp.sum(upper, axis=0)

        _, up_sum = lax.scan(upward, reflect_up, (diffuse, scattered), reverse=True)
        floor_sum = jnp.sum(beam_floor + spread_floor, axis=0)
        balance = jnp.concatenate([down_sum - up_sum, (floor_sum - jnp.sum(reflect_up, axis=0))[None]], axis=0)
        return balance[:-1] - balance[1:], floor_sum

    heating_parts, floor_parts = lax.map(one_block, (k_short.reshape(-1, block_size, k_short.shape[1]), solar_flux.reshape(-1, block_size)))
    return jnp.sum(heating_parts, axis=0) / gpoints, jnp.sum(floor_parts, axis=0) / gpoints


def reference(dyn_state, span_map, sunlit, coszen, albedo, ground_temp, aerosol, k_long, planck, k_short, solar_flux):
    blocks = N_GX * N_GY
    span_state = jnp.zeros_like(dyn_state).at[:, :, span_map].set(dyn_state)
    all_fields = jnp.concatenate([span_state, aerosol], axis=0)
    grouped = all_fields.reshape(NFIELD + NAER, LEV, blocks, COL_DEV).transpose(2, 0, 1, 3)

    def column_block(pieces):
        fields, cosine, albedo_part, ground_part, lit_part = pieces
        heat_lw, floor_lw = longwave(fields, k_long, planck, ground_part)
        heat_sw, floor_sw = shortwave(fields, k_short, solar_flux, cosine, albedo_part)
        lit_wide = lit_part.astype(jnp.float32)
        total_heat = heat_lw + heat_sw * lit_wide[None, :]
        return total_heat, jnp.stack([floor_lw, floor_sw * lit_wide], axis=0)

    heat_parts, floor_parts = lax.map(column_block, (grouped, coszen.reshape(blocks, COL_DEV), albedo.reshape(blocks, COL_DEV), ground_temp.reshape(blocks, COL_DEV), sunlit.reshape(blocks, COL_DEV)))
    heat_span = heat_parts.transpose(1, 0, 2).reshape(LEV, NCOL)
    surface = floor_parts.transpose(1, 0, 2).reshape(2, NCOL)
    heating = heat_span[:, span_map]
    return heating, surface
```

```python
import functools

import jax
import jax.numpy as jnp
from jax import lax
from jax.experimental import pallas as pl
from jax.experimental.pallas import tpu as pltpu
from jax.sharding import PartitionSpec as P

AXES = ("gx", "gy")
DIFFUSE = 1.66
SCATTER = 0.3
SW_DEPTH = 2.0
LOG2E = 1.4426950408889634
CAP = 4
BF16 = jnp.bfloat16
F32 = jnp.float32
NT = (((1,), (1,)), ((), ()))
TN = (((0,), (0,)), ((), ()))
MIB = 1 << 20


def onehot(mask):
    return jnp.where(mask, 1.0, 0.0).astype(BF16)


def halves(x):
    high = x.astype(BF16)
    return high, (x - high.astype(F32)).astype(BF16)


def softplus2(u):
    return jnp.maximum(u, jnp.log2(1.0 + jnp.exp2(jnp.minimum(u, 126.0))))


def pack_kernel(me_ref, map_ref, dyn_ref, out_ref, pick_ref, meta_ref, rows_ref):
    devices = out_ref.shape[0] // (2 * CAP)
    columns = map_ref.shape[1]
    step = pl.program_id(0)
    last = pl.num_programs(0) - 1

    @pl.when(step == 0)
    def _():
        where_to = map_ref[...]
        target = where_to // columns
        slot = where_to % columns
        same = target == lax.broadcasted_iota(jnp.int32, (devices, columns), 0)
        earlier = onehot(
            lax.broadcasted_iota(jnp.int32, (columns, columns), 0)
            < lax.broadcasted_iota(jnp.int32, (columns, columns), 1)
        )
        before = jnp.dot(onehot(same), earlier, preferred_element_type=F32)
        rank = jnp.sum(jnp.where(same, before, 0.0), axis=0, keepdims=True).astype(jnp.int32)
        rank = jnp.where(target == me_ref[0], CAP, rank)
        for place in range(CAP):
            pick_ref[place * devices : (place + 1) * devices, :] = onehot(same & (rank == place))
        line = lax.broadcasted_iota(jnp.int32, (128, columns), 0)
        mark = slot + 1
        meta = jnp.where(line == 0, mark // 2, jnp.where(line == 1, mark % 2, 0))
        meta_ref[...] = meta.astype(F32).astype(BF16)

    def put(part, half):
        moved = lax.dot_general(pick_ref[...], part, NT, preferred_element_type=F32)
        for place in range(CAP):
            rows_ref[pl.ds(place * 2 + half, devices, stride=2 * CAP), :] = moved[
                place * devices : (place + 1) * devices
            ]

    @pl.when(step < last)
    def _():
        for half in range(2):
            put(dyn_ref[:, half * 32 : half * 32 + 32, :].reshape(128, columns), half)

    @pl.when(step == last)
    def _():
        for half in range(2):
            put(meta_ref[...], half)

    out_ref[...] = rows_ref[...].astype(BF16)


def pack(me, map_row, dyn_state, devices):
    fields, levels, columns = dyn_state.shape
    steps = fields // 4
    return pl.pallas_call(
        pack_kernel,
        grid=(steps + 1,),
        in_specs=[
            pl.BlockSpec(memory_space=pltpu.SMEM),
            pl.BlockSpec((1, columns), lambda i: (0, 0)),
            pl.BlockSpec((4, levels, columns), lambda i: (jnp.minimum(i, steps - 1), 0, 0)),
        ],
        out_specs=[
            pl.BlockSpec((devices * CAP * 2, 128), lambda i: (0, i)),
            pl.BlockSpec((devices * CAP, columns), lambda i: (0, 0)),
        ],
        out_shape=[
            jax.ShapeDtypeStruct((devices * CAP * 2, (steps + 1) * 128), BF16),
            jax.ShapeDtypeStruct((devices * CAP, columns), BF16),
        ],
        scratch_shapes=[
            pltpu.VMEM((128, columns), BF16),
            pltpu.VMEM((devices * CAP * 2, 128), F32),
        ],
        compiler_params=pltpu.CompilerParams(vmem_limit_bytes=32 * MIB),
        cost_estimate=pl.CostEstimate(
            flops=2 * fields * levels * columns * devices * CAP, bytes_accessed=6 * MIB, transcendentals=0
        ),
        name="pack",
    )(me, map_row, dyn_state)


def base_kernel(me_ref, map_ref, dyn_ref, aer_ref, out_ref, pick_ref, rows_ref):
    fields, depth, columns = dyn_ref.shape
    extra = aer_ref.shape[0]
    first = out_ref.shape[1] - 64

    @pl.when(pl.program_id(0) == 0)
    def _():
        goal = lax.broadcasted_iota(jnp.int32, (columns, columns), 0) + me_ref[0] * columns
        pick_ref[...] = onehot(map_ref[...] == goal)

    kept = lax.dot_general(
        dyn_ref[...].reshape(fields * depth, columns), pick_ref[...], NT, preferred_element_type=F32
    )
    tall = fields * depth
    more = aer_ref[...].reshape(extra * depth, columns).astype(F32)
    for tile in range(columns // 128):
        lanes = slice(tile * 128, tile * 128 + 128)
        rows_ref[tile, :tall, :] = kept[:, lanes]
        rows_ref[tile, tall:, :] = more[:, lanes]
    for tile in range(columns // 128):
        lanes = slice(tile * 128, tile * 128 + 128)
        for level in range(depth):
            own = rows_ref[tile, pl.ds(level, fields, stride=depth), :]
            out_ref[level, :first, lanes] = jnp.concatenate(
                [own, jnp.zeros((first - fields, 128), F32)], axis=0
            ).astype(BF16)
            more = rows_ref[tile, pl.ds(tall + level, extra, stride=depth), :]
            out_ref[level, first:, lanes] = jnp.concatenate(
                [more, jnp.zeros((64 - extra, 128), F32)], axis=0
            ).astype(BF16)


def base(me, map_row, dyn_state, aerosol):
    fields, levels, columns = dyn_state.shape
    extra = aerosol.shape[0]
    depth = 16
    return pl.pallas_call(
        base_kernel,
        grid=(levels // depth,),
        in_specs=[
            pl.BlockSpec(memory_space=pltpu.SMEM),
            pl.BlockSpec((1, columns), lambda i: (0, 0)),
            pl.BlockSpec((fields, depth, columns), lambda i: (0, i, 0)),
            pl.BlockSpec((extra, depth, columns), lambda i: (0, i, 0)),
        ],
        out_specs=pl.BlockSpec((depth, 112, columns), lambda i: (i, 0, 0)),
        out_shape=jax.ShapeDtypeStruct((levels, 112, columns), BF16),
        scratch_shapes=[
            pltpu.VMEM((columns, columns), BF16),
            pltpu.VMEM((columns // 128, (fields + extra) * depth, 128), F32),
        ],
        compiler_params=pltpu.CompilerParams(vmem_limit_bytes=48 * MIB),
        cost_estimate=pl.CostEstimate(
            flops=2 * fields * levels * columns * columns, bytes_accessed=14 * MIB, transcendentals=0
        ),
        name="base",
    )(me, map_row, dyn_state, aerosol)


def flux_kernel(
    recv_hbm,
    base_hbm,
    k_ref,
    planck_ref,
    solar_ref,
    side_ref,
    heat_ref,
    surface_ref,
    back_ref,
    recv_ref,
    field_ref,
    pick_ref,
    state_ref,
    warm_ref,
    trans_ref,
    down_ref,
    beam_ref,
    diff_ref,
    up_ref,
    spread_ref,
    net_lw_ref,
    net_sw_ref,
    sems,
):
    rows = recv_ref.shape[0]
    devices = rows // (2 * CAP)
    levels, depth, columns = field_ref.shape
    glw = planck_ref.shape[0]
    gsw = solar_ref.shape[0]
    span = trans_ref.shape[2]
    tall = state_ref.shape[1]
    fields = tall // 32

    recv_copy = pltpu.make_async_copy(recv_hbm, recv_ref, sems.at[0])
    base_copy = pltpu.make_async_copy(base_hbm, field_ref, sems.at[1])
    recv_copy.start()
    base_copy.start()

    recv_copy.wait()
    mark = recv_ref[:, tall : tall + 128].astype(F32)
    mark = (mark[:, 0:1] * 2.0 + mark[:, 1:2]).astype(jnp.int32)
    half_of = lax.broadcasted_iota(jnp.int32, (rows, 1), 0) % 2
    for half in range(2):
        key = jnp.where(half_of == half, mark, 0)
        for tile in range(0, columns, 128):
            lane = lax.broadcasted_iota(jnp.int32, (rows, 128), 1) + (tile + 1)
            pick_ref[:, half * columns + tile : half * columns + tile + 128] = onehot(key == lane)
    for tile in range(0, tall, 128):
        moved = lax.dot_general(
            recv_ref[:, tile : tile + 128], pick_ref[...], TN, preferred_element_type=F32
        )
        for part in range(2 * columns // 128):
            state_ref[part, tile : tile + 128, :] = moved[:, part * 128 : part * 128 + 128]
    base_copy.wait()

    for half in range(2):

        def place_level(inner, _, half=half):
            level = half * 32 + inner
            here = jnp.concatenate(
                [
                    state_ref[half * (columns // 128) + part, pl.ds(inner, fields, stride=32), :]
                    for part in range(columns // 128)
                ],
                axis=1,
            )
            here = here + field_ref[level, :48, :].astype(F32)[:fields]
            warmth = softplus2(jnp.broadcast_to(here[0:1], (8, columns)) * LOG2E)
            warm_ref[level] = warmth * (1.0 / LOG2E)
            field_ref[level, :48, :] = jnp.concatenate(
                [here, jnp.zeros((48 - fields, columns), F32)], axis=0
            ).astype(BF16)
            return 0

        lax.fori_loop(0, 32, place_level, 0)

    side = side_ref[...]
    cosine, albedo, ground, lit = (side[i : i + 1] for i in range(4))
    slant = (-SW_DEPTH / levels) / cosine
    skin = softplus2(ground * LOG2E) * (1.0 / LOG2E)
    tiles = span // 128
    for start in range(0, columns, span):
        lanes = [slice(start + 128 * t, start + 128 * t + 128) for t in range(tiles)]
        cuts = [slice(128 * t, 128 * t + 128) for t in range(tiles)]
        down_ref[0] = jnp.zeros((glw, span), F32)
        spread_ref[...] = jnp.zeros((gsw, span), F32)
        for t in range(tiles):
            beam_ref[0, :, cuts[t]] = SCATTER * solar_ref[...]

        def descend(level, _):
            depth_of = jnp.dot(
                k_ref[...], field_ref[level, :, start : start + span], preferred_element_type=F32
            )
            for t in range(tiles):
                warm = warm_ref[level, :, lanes[t]]
                slope = jnp.broadcast_to(slant[:, lanes[t]], (8, 128))
                for g in range(0, glw, 8):
                    u = depth_of[g : g + 8, cuts[t]] * LOG2E
                    tau = jnp.log2(1.0 + jnp.exp2(jnp.minimum(u, 126.0)))
                    trans = jnp.exp2(tau * (-DIFFUSE))
                    trans_ref[level, g : g + 8, cuts[t]] = trans
                    down = down_ref[level, g : g + 8, cuts[t]]
                    down_ref[level + 1, g : g + 8, cuts[t]] = warm + trans * (down - warm)
                sum_beam = jnp.zeros((8, 128), F32)
                sum_spread = jnp.zeros((8, 128), F32)
                for g in range(0, gsw, 8):
                    u = depth_of[glw + g : glw + g + 8, cuts[t]] * LOG2E
                    tau = jnp.maximum(u, jnp.log2(1.0 + jnp.exp2(jnp.minimum(u, 126.0))))
                    direct = jnp.exp2(tau * slope)
                    diffuse = jnp.exp2(tau * (-DIFFUSE * SW_DEPTH / levels))
                    diff_ref[level, g : g + 8, cuts[t]] = diffuse
                    beam = beam_ref[level, g : g + 8, cuts[t]]
                    lower = direct * beam
                    beam_ref[level + 1, g : g + 8, cuts[t]] = lower
                    spread = spread_ref[g : g + 8, cuts[t]]
                    spread_ref[g : g + 8, cuts[t]] = diffuse * spread + (beam - lower)
                    sum_beam = sum_beam + beam
                    sum_spread = sum_spread + spread
                net_sw_ref[level, :, lanes[t]] = sum_beam * (1.0 / SCATTER) + sum_spread
            return 0

        lax.fori_loop(0, levels, descend, 0)

        for t in range(tiles):
            sum_net = jnp.zeros((8, 128), F32)
            ground_up = jnp.broadcast_to(skin[:, lanes[t]], (8, 128))
            sum_floor = jnp.zeros((8, 128), F32)
            for g in range(0, glw, 8):
                floor = planck_ref[g : g + 8, :] * down_ref[levels, g : g + 8, cuts[t]]
                sum_floor = sum_floor + floor
                sum_net = sum_net + (floor - planck_ref[g : g + 8, :] * ground_up)
                up_ref[g : g + 8, cuts[t]] = ground_up
            net_lw_ref[levels, :, lanes[t]] = sum_net
            surface_ref[0:1, lanes[t]] = jnp.sum(sum_floor, axis=0, keepdims=True) * (1.0 / glw)
            bright = jnp.broadcast_to(albedo[:, lanes[t]], (8, 128))
            sum_floor = jnp.zeros((8, 128), F32)
            for g in range(0, gsw, 8):
                floor = beam_ref[levels, g : g + 8, cuts[t]] * (1.0 / SCATTER) + spread_ref[g : g + 8, cuts[t]]
                sum_floor = sum_floor + floor
                spread_ref[g : g + 8, cuts[t]] = bright * floor
            net_sw_ref[levels, :, lanes[t]] = sum_floor - bright * sum_floor
            surface_ref[1:2, lanes[t]] = jnp.sum(sum_floor, axis=0, keepdims=True) * (
                lit[:, lanes[t]] * cosine[:, lanes[t]] * (1.0 / gsw)
            )

        def ascend(step, _):
            level = levels - 1 - step
            for t in range(tiles):
                warm = warm_ref[level, :, lanes[t]]
                sum_net = jnp.zeros((8, 128), F32)
                for g in range(0, glw, 8):
                    upper = warm + trans_ref[level, g : g + 8, cuts[t]] * (up_ref[g : g + 8, cuts[t]] - warm)
                    up_ref[g : g + 8, cuts[t]] = upper
                    sum_net = sum_net + planck_ref[g : g + 8, :] * (
                        down_ref[level, g : g + 8, cuts[t]] - upper
                    )
                net_lw_ref[level, :, lanes[t]] = sum_net
                sum_up = jnp.zeros((8, 128), F32)
                for g in range(0, gsw, 8):
                    upper = diff_ref[level, g : g + 8, cuts[t]] * spread_ref[g : g + 8, cuts[t]] + (
                        beam_ref[level, g : g + 8, cuts[t]] - beam_ref[level + 1, g : g + 8, cuts[t]]
                    )
                    spread_ref[g : g + 8, cuts[t]] = upper
                    sum_up = sum_up + upper
                net_sw_ref[level, :, lanes[t]] = net_sw_ref[level, :, lanes[t]] - sum_up
            return 0

        lax.fori_loop(0, levels, ascend, 0)

    net_lw = jnp.sum(net_lw_ref[...], axis=1)
    net_sw = jnp.sum(net_sw_ref[...], axis=1)
    heat = (net_lw[:levels] - net_lw[1 : levels + 1]) * (1.0 / glw) + (
        net_sw[:levels] - net_sw[1 : levels + 1]
    ) * (lit * cosine * (1.0 / gsw))
    heat_ref[...] = heat

    twice = jnp.concatenate([heat, heat], axis=0)
    high, low = halves(twice)
    picked = pick_ref[:, :columns]
    state_ref[0, :rows, :] = lax.dot_general(picked, high, NT, preferred_element_type=F32) + lax.dot_general(
        picked, low, NT, preferred_element_type=F32
    )
    left = lax.broadcasted_iota(jnp.int32, (devices, 128), 1) < levels
    for pair in range(2):
        even = state_ref[0, pl.ds(4 * pair, devices, stride=8), :]
        odd = state_ref[0, pl.ds(4 * pair + 2, devices, stride=8), :]
        back_ref[pl.ds(pair, devices, stride=2), :] = jnp.where(left, even, odd)


def flux(recv, fields_base, coefficients, planck, solar, side, fields):
    rows, width = recv.shape
    levels, depth, columns = fields_base.shape
    glw, gsw = planck.shape[0], solar.shape[0]
    span = 256
    devices = rows // (2 * CAP)
    whole = pl.BlockSpec(memory_space=pltpu.VMEM)
    count = (glw + gsw) * levels * columns
    return pl.pallas_call(
        flux_kernel,
        in_specs=[pl.BlockSpec(memory_space=pl.ANY)] * 2 + [whole] * 4,
        out_specs=[whole] * 3,
        out_shape=[
            jax.ShapeDtypeStruct((levels, columns), F32),
            jax.ShapeDtypeStruct((2, columns), F32),
            jax.ShapeDtypeStruct((devices * 2, 128), F32),
        ],
        scratch_shapes=[
            pltpu.VMEM((rows, width), BF16),
            pltpu.VMEM((levels, depth, columns), BF16),
            pltpu.VMEM((rows, 2 * columns), BF16),
            pltpu.VMEM((2 * columns // 128, fields * 32, 128), F32),
            pltpu.VMEM((levels, 8, columns), F32),
            pltpu.VMEM((levels, glw, span), F32),
            pltpu.VMEM((levels + 1, glw, span), F32),
            pltpu.VMEM((levels + 1, gsw, span), F32),
            pltpu.VMEM((levels, gsw, span), F32),
            pltpu.VMEM((glw, span), F32),
            pltpu.VMEM((gsw, span), F32),
            pltpu.VMEM((levels + 1, 8, columns), F32),
            pltpu.VMEM((levels + 1, 8, columns), F32),
            pltpu.SemaphoreType.DMA((2,)),
        ],
        compiler_params=pltpu.CompilerParams(vmem_limit_bytes=58 * MIB),
        cost_estimate=pl.CostEstimate(flops=250 * count, bytes_accessed=12 * MIB, transcendentals=4 * count),
        name="flux",
    )(recv, fields_base, coefficients, planck, solar, side)


def local_kernel(me_ref, map_ref, heat_ref, out_ref):
    columns = map_ref.shape[1]
    goal = lax.broadcasted_iota(jnp.int32, (columns, columns), 0) + me_ref[0] * columns
    stay = onehot(map_ref[...] == goal)
    high, low = halves(heat_ref[...])
    out_ref[...] = jnp.dot(high, stay, preferred_element_type=F32) + jnp.dot(
        low, stay, preferred_element_type=F32
    )


def unpack_kernel(local_ref, pick_ref, back_ref, out_ref):
    devices = back_ref.shape[0] // 2
    levels = local_ref.shape[0]
    total = local_ref[...]
    for pair in range(2):
        high, low = halves(back_ref[pl.ds(pair, devices, stride=2), :])
        for side in range(2):
            place = 2 * pair + side
            pick = pick_ref[place * devices : (place + 1) * devices, :]
            part = lax.dot_general(high, pick, TN, preferred_element_type=F32) + lax.dot_general(
                low, pick, TN, preferred_element_type=F32
            )
            total = total + part[side * levels : (side + 1) * levels]
    out_ref[...] = total


def shards(
    dyn_state,
    span_map,
    sunlit,
    coszen,
    albedo,
    ground_temp,
    aerosol,
    k_long,
    planck,
    k_short,
    solar_flux,
):
    fields, levels, columns = dyn_state.shape
    devices = lax.axis_size("gx") * lax.axis_size("gy")
    me = lax.axis_index(AXES).astype(jnp.int32).reshape(1)
    map_row = span_map.reshape(1, columns)
    swap = functools.partial(lax.all_to_all, axis_name=AXES, split_axis=0, concat_axis=0, tiled=True)

    outgoing, pick = pack(me, map_row, dyn_state, devices)
    width = outgoing.shape[1]
    recv = swap(outgoing.reshape(devices, 2 * CAP, width)).reshape(devices * 2 * CAP, width)
    fields_base = base(me, map_row, dyn_state, aerosol)

    both = jnp.concatenate([k_long, k_short], axis=0)
    gap = lambda n: jnp.zeros((both.shape[0], n), both.dtype)
    coefficients = jnp.concatenate(
        [both[:, :fields], gap(48 - fields), both[:, fields:], gap(64 - aerosol.shape[0])], axis=1
    )
    side = jnp.stack([coszen, albedo, ground_temp, sunlit.astype(F32)], axis=0)
    wide = lambda x: jnp.broadcast_to(x[:, None], (x.shape[0], 128))
    heat, surface, back = flux(
        recv, fields_base, coefficients, wide(planck), wide(solar_flux), side, fields
    )

    returned = swap(back.reshape(devices, 2, 128)).reshape(devices * 2, 128)
    whole = pl.BlockSpec(memory_space=pltpu.VMEM)
    local = pl.pallas_call(
        local_kernel,
        in_specs=[pl.BlockSpec(memory_space=pltpu.SMEM), whole, whole],
        out_specs=whole,
        out_shape=jax.ShapeDtypeStruct((levels, columns), F32),
        cost_estimate=pl.CostEstimate(
            flops=4 * levels * columns * columns, bytes_accessed=MIB, transcendentals=0
        ),
        name="local",
    )(me, map_row, heat)
    heating = pl.pallas_call(
        unpack_kernel,
        in_specs=[whole] * 3,
        out_specs=whole,
        out_shape=jax.ShapeDtypeStruct((levels, columns), F32),
        cost_estimate=pl.CostEstimate(
            flops=8 * levels * columns * columns, bytes_accessed=MIB, transcendentals=0
        ),
        name="unpack",
    )(local, pick, returned)
    return heating, surface


def solution(mesh):
    cols = P(AXES)
    in_specs = (
        P(None, None, AXES),
        cols,
        cols,
        cols,
        cols,
        cols,
        P(None, None, AXES),
        P(),
        P(),
        P(),
        P(),
    )
    out_specs = (P(None, AXES), P(None, AXES))
    return jax.shard_map(shards, mesh=mesh, in_specs=in_specs, out_specs=out_specs, check_vma=False)
```

```python
import functools

import jax
import jax.numpy as jnp
from jax import lax
from jax.experimental import pallas as pl
from jax.experimental.pallas import tpu as pltpu
from jax.sharding import PartitionSpec as P

AXES = ("gx", "gy")
DIFFUSE = 1.66
SCATTER = 0.3
SW_DEPTH = 2.0
LOG2E = 1.4426950408889634
CAP = 4
BF16 = jnp.bfloat16
F32 = jnp.float32
NT = (((1,), (1,)), ((), ()))
TN = (((0,), (0,)), ((), ()))
MIB = 1 << 20


def onehot(mask):
    return jnp.where(mask, 1.0, 0.0).astype(BF16)


def halves(x):
    high = x.astype(BF16)
    return high, (x - high.astype(F32)).astype(BF16)


def softplus2(u):
    return jnp.maximum(u, jnp.log2(1.0 + jnp.exp2(jnp.minimum(u, 126.0))))


def pack_kernel(me_ref, map_ref, dyn_ref, out_ref, pick_ref, meta_ref, rows_ref):
    devices = out_ref.shape[0] // (2 * CAP)
    columns = map_ref.shape[1]
    step = pl.program_id(0)
    last = pl.num_programs(0) - 1

    @pl.when(step == 0)
    def _():
        where_to = map_ref[...]
        target = where_to // columns
        slot = where_to % columns
        same = target == lax.broadcasted_iota(jnp.int32, (devices, columns), 0)
        earlier = onehot(
            lax.broadcasted_iota(jnp.int32, (columns, columns), 0)
            < lax.broadcasted_iota(jnp.int32, (columns, columns), 1)
        )
        before = jnp.dot(onehot(same), earlier, preferred_element_type=F32)
        rank = jnp.sum(jnp.where(same, before, 0.0), axis=0, keepdims=True).astype(jnp.int32)
        rank = jnp.where(target == me_ref[0], CAP, rank)
        for place in range(CAP):
            pick_ref[place * devices : (place + 1) * devices, :] = onehot(same & (rank == place))
        line = lax.broadcasted_iota(jnp.int32, (128, columns), 0)
        mark = slot + 1
        meta = jnp.where(line == 0, mark // 2, jnp.where(line == 1, mark % 2, 0))
        meta_ref[...] = meta.astype(F32).astype(BF16)

    def put(part, half):
        moved = lax.dot_general(pick_ref[...], part, NT, preferred_element_type=F32)
        for place in range(CAP):
            rows_ref[pl.ds(place * 2 + half, devices, stride=2 * CAP), :] = moved[
                place * devices : (place + 1) * devices
            ]

    @pl.when(step < last)
    def _():
        for half in range(2):
            put(dyn_ref[:, half * 32 : half * 32 + 32, :].reshape(128, columns), half)

    @pl.when(step == last)
    def _():
        for half in range(2):
            put(meta_ref[...], half)

    out_ref[...] = rows_ref[...].astype(BF16)


def pack(me, map_row, dyn_state, devices):
    fields, levels, columns = dyn_state.shape
    steps = fields // 4
    return pl.pallas_call(
        pack_kernel,
        grid=(steps + 1,),
        in_specs=[
            pl.BlockSpec(memory_space=pltpu.SMEM),
            pl.BlockSpec((1, columns), lambda i: (0, 0)),
            pl.BlockSpec((4, levels, columns), lambda i: (jnp.minimum(i, steps - 1), 0, 0)),
        ],
        out_specs=[
            pl.BlockSpec((devices * CAP * 2, 128), lambda i: (0, i)),
            pl.BlockSpec((devices * CAP, columns), lambda i: (0, 0)),
        ],
        out_shape=[
            jax.ShapeDtypeStruct((devices * CAP * 2, (steps + 1) * 128), BF16),
            jax.ShapeDtypeStruct((devices * CAP, columns), BF16),
        ],
        scratch_shapes=[
            pltpu.VMEM((128, columns), BF16),
            pltpu.VMEM((devices * CAP * 2, 128), F32),
        ],
        compiler_params=pltpu.CompilerParams(vmem_limit_bytes=56 * MIB),
        cost_estimate=pl.CostEstimate(
            flops=2 * fields * levels * columns * devices * CAP, bytes_accessed=6 * MIB, transcendentals=0
        ),
        name="pack",
    )(me, map_row, dyn_state)


def base_kernel(
    me_ref,
    map_ref,
    dyn_ref,
    aer_ref,
    long_ref,
    short_ref,
    planck_ref,
    solar_ref,
    out_ref,
    warm_ref,
    k_ref,
    weight_ref,
    pick_ref,
    rows_ref,
):
    fields, depth, columns = dyn_ref.shape
    extra = aer_ref.shape[0]
    tiles = columns // 128
    first = 48
    glw, gsw = long_ref.shape[0], short_ref.shape[0]

    @pl.when(pl.program_id(0) == 0)
    def _():
        goal = lax.broadcasted_iota(jnp.int32, (columns, columns), 0) + me_ref[0] * columns
        pick_ref[...] = onehot(map_ref[...] == goal)
        k_ref[...] = jnp.zeros(k_ref.shape, BF16)
        for coefficients, start in ((long_ref[...], 0), (short_ref[...], glw)):
            rows = slice(start, start + coefficients.shape[0])
            k_ref[rows, :fields] = coefficients[:, :fields]
            k_ref[rows, 48 : 48 + fields] = coefficients[:, :fields]
            k_ref[rows, 96 : 96 + extra] = coefficients[:, fields:]
        square = lax.broadcasted_iota(jnp.int32, (128, 128), 0) == lax.broadcasted_iota(
            jnp.int32, (128, 128), 1
        )
        for source, start in ((planck_ref[...], 0), (solar_ref[...], glw)):
            size = source.shape[1]
            picked = jnp.where(square[:size, :size], source, 0.0)
            weight_ref[start : start + size, :] = jnp.broadcast_to(
                jnp.sum(picked, axis=1, keepdims=True), (size, 128)
            )

    kept = lax.dot_general(
        dyn_ref[...].reshape(fields * depth, columns), pick_ref[...], NT, preferred_element_type=F32
    )
    warm_ref[...] = kept[:depth]
    tall = fields * depth
    more = aer_ref[...].reshape(extra * depth, columns).astype(F32)
    for tile in range(tiles):
        lanes = slice(tile * 128, tile * 128 + 128)
        rows_ref[tile, :tall, :] = kept[:, lanes]
        rows_ref[tile, tall:, :] = more[:, lanes]
    for tile in range(tiles):
        for level in range(depth):
            own = rows_ref[tile, pl.ds(level, fields, stride=depth), :]
            out_ref[tile, level, :first, :] = jnp.concatenate(
                [own, jnp.zeros((first - fields, 128), F32)], axis=0
            ).astype(BF16)
            aero = rows_ref[tile, pl.ds(tall + level, extra, stride=depth), :]
            out_ref[tile, level, first:, :] = jnp.concatenate(
                [aero, jnp.zeros((64 - extra, 128), F32)], axis=0
            ).astype(BF16)


def base(me, map_row, dyn_state, aerosol, k_long, k_short, planck, solar):
    fields, levels, columns = dyn_state.shape
    extra = aerosol.shape[0]
    glw, gsw = k_long.shape[0], k_short.shape[0]
    depth = 16
    tiles = columns // 128
    fixed = lambda *shape: pl.BlockSpec(shape, lambda i: (0,) * len(shape))
    return pl.pallas_call(
        base_kernel,
        grid=(levels // depth,),
        in_specs=[
            pl.BlockSpec(memory_space=pltpu.SMEM),
            fixed(1, columns),
            pl.BlockSpec((fields, depth, columns), lambda i: (0, i, 0)),
            pl.BlockSpec((extra, depth, columns), lambda i: (0, i, 0)),
            fixed(*k_long.shape),
            fixed(*k_short.shape),
            fixed(1, glw),
            fixed(1, gsw),
        ],
        out_specs=[
            pl.BlockSpec((tiles, depth, 112, 128), lambda i: (0, i, 0, 0)),
            pl.BlockSpec((depth, columns), lambda i: (i, 0)),
            fixed(glw + gsw, 160),
            fixed(glw + gsw, 128),
        ],
        out_shape=[
            jax.ShapeDtypeStruct((tiles, levels, 112, 128), BF16),
            jax.ShapeDtypeStruct((levels, columns), F32),
            jax.ShapeDtypeStruct((glw + gsw, 160), BF16),
            jax.ShapeDtypeStruct((glw + gsw, 128), F32),
        ],
        scratch_shapes=[
            pltpu.VMEM((columns, columns), BF16),
            pltpu.VMEM((tiles, (fields + extra) * depth, 128), F32),
        ],
        compiler_params=pltpu.CompilerParams(vmem_limit_bytes=56 * MIB),
        cost_estimate=pl.CostEstimate(
            flops=2 * fields * levels * columns * columns, bytes_accessed=14 * MIB, transcendentals=0
        ),
        name="base",
    )(me, map_row, dyn_state, aerosol, k_long, k_short, planck.reshape(1, glw), solar.reshape(1, gsw))


def flux_kernel(
    recv_hbm,
    base_hbm,
    kept_ref,
    k_ref,
    weight_ref,
    cos_ref,
    albedo_ref,
    ground_ref,
    lit_ref,
    heat_ref,
    surface_ref,
    back_ref,
    recv_ref,
    base_ref,
    pick_ref,
    state_ref,
    warm_ref,
    trans_refs,
    down_refs,
    beam_refs,
    diff_refs,
    depth_refs,
    up_ref,
    spread_ref,
    return_ref,
    net_lw_ref,
    net_sw_ref,
    sems,
):
    rows = recv_ref.shape[0]
    devices = rows // (2 * CAP)
    tiles, levels, _, _ = base_ref.shape
    columns = 128 * tiles
    glw, gsw = up_ref.shape[0], return_ref.shape[0]
    tall = state_ref.shape[1]
    fields = tall // 32
    pairs = levels // 2

    recv_copy = pltpu.make_async_copy(recv_hbm, recv_ref, sems.at[0])
    base_copy = pltpu.make_async_copy(base_hbm, base_ref, sems.at[1])
    recv_copy.start()
    base_copy.start()

    recv_copy.wait()
    mark = recv_ref[:, tall : tall + 128].astype(F32)
    mark = (mark[:, 0:1] * 2.0 + mark[:, 1:2]).astype(jnp.int32)
    half_of = lax.broadcasted_iota(jnp.int32, (rows, 1), 0) % 2
    for half in range(2):
        key = jnp.where(half_of == half, mark, 0)
        for tile in range(0, columns, 128):
            lane = lax.broadcasted_iota(jnp.int32, (rows, 128), 1) + (tile + 1)
            pick_ref[:, half * columns + tile : half * columns + tile + 128] = onehot(key == lane)
    for tile in range(0, tall, 128):
        moved = lax.dot_general(
            recv_ref[:, tile : tile + 128], pick_ref[...], TN, preferred_element_type=F32
        )
        for part in range(2 * tiles):
            state_ref[part, tile : tile + 128, :] = moved[:, part * 128 : part * 128 + 128]

    for part in range(2 * tiles):
        half, tile = part // tiles, part % tiles
        lanes = slice(tile * 128, tile * 128 + 128)
        cold = state_ref[part, :32, :] + kept_ref[half * 32 : half * 32 + 32, lanes]
        warmth = softplus2(cold * LOG2E) * (1.0 / LOG2E)
        for inner in range(32):
            warm_ref[half * 32 + inner, :, lanes] = jnp.broadcast_to(warmth[inner : inner + 1], (8, 128))
    base_copy.wait()

    cosine, albedo, ground = cos_ref[...], albedo_ref[...], ground_ref[...]
    lit = lit_ref[...].astype(F32)
    slant = (-SW_DEPTH / levels) / cosine
    skin = softplus2(ground * LOG2E) * (1.0 / LOG2E)
    lanes_of = lambda tile: slice(tile * 128, tile * 128 + 128)

    def absorb(pair, tile):
        half = pair // (pairs // 2)
        inner = 2 * pair - 32 * half
        both = [
            state_ref[half * tiles + tile, pl.ds(inner + e, fields, stride=32), :] for e in range(2)
        ]
        here = jnp.concatenate(
            [jnp.concatenate(both, axis=1), jnp.zeros((48 - fields, 256), F32)], axis=0
        ).astype(BF16)
        rest = jnp.concatenate([base_ref[tile, 2 * pair + e] for e in range(2)], axis=1)
        return jnp.dot(k_ref[...], jnp.concatenate([here, rest], axis=0), preferred_element_type=F32)

    def descend(pair, tile, depth_ref):
        trans_ref, down_ref = trans_refs[tile % 2], down_refs[tile % 2]
        beam_ref, diff_ref = beam_refs[tile % 2], diff_refs[tile % 2]
        level = 2 * pair
        warm = [warm_ref[level + e, :, lanes_of(tile)] for e in range(2)]
        for g in range(0, glw, 8):
            down = down_ref[level, g : g + 8, :]
            for e in range(2):
                u = depth_ref[g : g + 8, 128 * e : 128 * e + 128] * LOG2E
                tau = jnp.log2(1.0 + jnp.exp2(jnp.minimum(u, 126.0)))
                trans = jnp.exp2(tau * (-DIFFUSE))
                trans_ref[level + e, g : g + 8, :] = trans
                down = warm[e] + trans * (down - warm[e])
                down_ref[level + e + 1, g : g + 8, :] = down
        slope = jnp.broadcast_to(slant[:, lanes_of(tile)], (8, 128))
        sum_beam = [jnp.zeros((8, 128), F32) for _ in range(2)]
        sum_spread = [jnp.zeros((8, 128), F32) for _ in range(2)]
        for g in range(0, gsw, 8):
            beam = beam_ref[level, g : g + 8, :]
            spread = spread_ref[g : g + 8, :]
            for e in range(2):
                u = depth_ref[glw + g : glw + g + 8, 128 * e : 128 * e + 128] * LOG2E
                tau = jnp.maximum(u, jnp.log2(1.0 + jnp.exp2(jnp.minimum(u, 126.0))))
                diffuse = jnp.exp2(tau * (-DIFFUSE * SW_DEPTH / levels))
                diff_ref[level + e, g : g + 8, :] = diffuse
                lower = jnp.exp2(tau * slope) * beam
                beam_ref[level + e + 1, g : g + 8, :] = lower
                sum_beam[e] = sum_beam[e] + beam
                sum_spread[e] = sum_spread[e] + spread
                spread = diffuse * spread + (beam - lower)
                beam = lower
            spread_ref[g : g + 8, :] = spread
        for e in range(2):
            net_sw_ref[level + e, :, lanes_of(tile)] = sum_beam[e] * (1.0 / SCATTER) + sum_spread[e]

    def ascend(pair, tile):
        trans_ref, down_ref = trans_refs[tile % 2], down_refs[tile % 2]
        beam_ref, diff_ref = beam_refs[tile % 2], diff_refs[tile % 2]
        level = 2 * pair
        warm = [warm_ref[level + e, :, lanes_of(tile)] for e in range(2)]
        total = [jnp.zeros((8, 128), F32) for _ in range(2)]
        for g in range(0, glw, 8):
            upper = up_ref[g : g + 8, :]
            weight = weight_ref[g : g + 8, :]
            for e in (1, 0):
                upper = warm[e] + trans_ref[level + e, g : g + 8, :] * (upper - warm[e])
                total[e] = total[e] + weight * (down_ref[level + e, g : g + 8, :] - upper)
            up_ref[g : g + 8, :] = upper
        for e in range(2):
            net_lw_ref[level + e, :, lanes_of(tile)] = total[e]
        total = [net_sw_ref[level + e, :, lanes_of(tile)] for e in range(2)]
        for g in range(0, gsw, 8):
            upper = return_ref[g : g + 8, :]
            lower = beam_ref[level + 2, g : g + 8, :]
            for e in (1, 0):
                beam = beam_ref[level + e, g : g + 8, :]
                upper = diff_ref[level + e, g : g + 8, :] * upper + (beam - lower)
                total[e] = total[e] - upper
                lower = beam
            return_ref[g : g + 8, :] = upper
        for e in range(2):
            net_sw_ref[level + e, :, lanes_of(tile)] = total[e]

    def turn(tile):
        lanes = lanes_of(tile)
        down_ref, beam_ref = down_refs[tile % 2], beam_refs[tile % 2]
        total = jnp.zeros((8, 128), F32)
        floor_total = jnp.zeros((8, 128), F32)
        upper = jnp.broadcast_to(skin[:, lanes], (8, 128))
        for g in range(0, glw, 8):
            weight = weight_ref[g : g + 8, :]
            floor = weight * down_ref[levels, g : g + 8, :]
            floor_total = floor_total + floor
            total = total + (floor - weight * upper)
            up_ref[g : g + 8, :] = upper
        net_lw_ref[levels, :, lanes] = total
        surface_ref[0:1, lanes] = jnp.sum(floor_total, axis=0, keepdims=True) * (1.0 / glw)
        bright = jnp.broadcast_to(albedo[:, lanes], (8, 128))
        floor_total = jnp.zeros((8, 128), F32)
        for g in range(0, gsw, 8):
            floor = beam_ref[levels, g : g + 8, :] * (1.0 / SCATTER) + spread_ref[g : g + 8, :]
            floor_total = floor_total + floor
            return_ref[g : g + 8, :] = bright * floor
        net_sw_ref[levels, :, lanes] = floor_total - bright * floor_total
        surface_ref[1:2, lanes] = jnp.sum(floor_total, axis=0, keepdims=True) * (
            lit[:, lanes] * cosine[:, lanes] * (1.0 / gsw)
        )

    depth_refs[0][...] = absorb(0, 0)
    for tile in range(tiles + 1):
        if tile < tiles:
            down_refs[tile % 2][0] = jnp.zeros((glw, 128), F32)
            spread_ref[...] = jnp.zeros((gsw, 128), F32)
            beam_refs[tile % 2][0] = SCATTER * weight_ref[glw:, :]

        def both_ways(step, _, tile=tile):
            for part in range(2):
                pair = 2 * step + part
                if tile < tiles:
                    over = pair == pairs - 1
                    following = jnp.where(over, 0, pair + 1)
                    following_tile = jnp.where(over, min(tile + 1, tiles - 1), tile)
                    depth_refs[1 - part][...] = absorb(following, following_tile)
                    descend(pair, tile, depth_refs[part])
                if tile > 0:
                    ascend(pairs - 1 - pair, tile - 1)
            return 0

        lax.fori_loop(0, pairs // 2, both_ways, 0, unroll=4)
        if tile < tiles:
            turn(tile)

    net_lw = jnp.sum(net_lw_ref[...], axis=1)
    net_sw = jnp.sum(net_sw_ref[...], axis=1)
    heat = (net_lw[:levels] - net_lw[1 : levels + 1]) * (1.0 / glw) + (
        net_sw[:levels] - net_sw[1 : levels + 1]
    ) * (lit * cosine * (1.0 / gsw))
    heat_ref[...] = heat

    twice = jnp.concatenate([heat, heat], axis=0)
    high, low = halves(twice)
    picked = pick_ref[:, :columns]
    state_ref[0, :rows, :] = lax.dot_general(picked, high, NT, preferred_element_type=F32) + lax.dot_general(
        picked, low, NT, preferred_element_type=F32
    )
    left = lax.broadcasted_iota(jnp.int32, (devices, 128), 1) < levels
    for pair in range(2):
        even = state_ref[0, pl.ds(4 * pair, devices, stride=8), :]
        odd = state_ref[0, pl.ds(4 * pair + 2, devices, stride=8), :]
        back_ref[pl.ds(pair, devices, stride=2), :] = jnp.where(left, even, odd)


def flux(recv, fields_base, kept, coefficients, weights, coszen, albedo, ground, sunlit, fields, glw):
    rows, width = recv.shape
    tiles, levels, depth, _ = fields_base.shape
    columns = 128 * tiles
    gsw = weights.shape[0] - glw
    devices = rows // (2 * CAP)
    whole = pl.BlockSpec(memory_space=pltpu.VMEM)
    count = (glw + gsw) * levels * columns
    twice = lambda *shape: [pltpu.VMEM(shape, F32)] * 2
    return pl.pallas_call(
        flux_kernel,
        in_specs=[pl.BlockSpec(memory_space=pl.ANY)] * 2 + [whole] * 7,
        out_specs=[whole] * 3,
        out_shape=[
            jax.ShapeDtypeStruct((levels, columns), F32),
            jax.ShapeDtypeStruct((2, columns), F32),
            jax.ShapeDtypeStruct((devices * 2, 128), F32),
        ],
        scratch_shapes=[
            pltpu.VMEM((rows, width), BF16),
            pltpu.VMEM((tiles, levels, depth, 128), BF16),
            pltpu.VMEM((rows, 2 * columns), BF16),
            pltpu.VMEM((2 * tiles, fields * 32, 128), F32),
            pltpu.VMEM((levels, 8, columns), F32),
            twice(levels, glw, 128),
            twice(levels + 1, glw, 128),
            twice(levels + 1, gsw, 128),
            twice(levels, gsw, 128),
            twice(glw + gsw, 256),
            pltpu.VMEM((glw, 128), F32),
            pltpu.VMEM((gsw, 128), F32),
            pltpu.VMEM((gsw, 128), F32),
            pltpu.VMEM((levels + 1, 8, columns), F32),
            pltpu.VMEM((levels + 1, 8, columns), F32),
            pltpu.SemaphoreType.DMA((2,)),
        ],
        compiler_params=pltpu.CompilerParams(vmem_limit_bytes=60 * MIB),
        cost_estimate=pl.CostEstimate(flops=250 * count, bytes_accessed=12 * MIB, transcendentals=4 * count),
        name="flux",
    )(recv, fields_base, kept, coefficients, weights, coszen, albedo, ground, sunlit)


def local_kernel(me_ref, map_ref, heat_ref, out_ref):
    columns = map_ref.shape[1]
    goal = lax.broadcasted_iota(jnp.int32, (columns, columns), 0) + me_ref[0] * columns
    stay = onehot(map_ref[...] == goal)
    high, low = halves(heat_ref[...])
    out_ref[...] = jnp.dot(high, stay, preferred_element_type=F32) + jnp.dot(
        low, stay, preferred_element_type=F32
    )


def unpack_kernel(local_ref, pick_ref, back_ref, out_ref):
    devices = back_ref.shape[0] // 2
    levels = local_ref.shape[0]
    total = local_ref[...]
    for pair in range(2):
        high, low = halves(back_ref[pl.ds(pair, devices, stride=2), :])
        for side in range(2):
            place = 2 * pair + side
            pick = pick_ref[place * devices : (place + 1) * devices, :]
            part = lax.dot_general(high, pick, TN, preferred_element_type=F32) + lax.dot_general(
                low, pick, TN, preferred_element_type=F32
            )
            total = total + part[side * levels : (side + 1) * levels]
    out_ref[...] = total


def shards(
    dyn_state,
    span_map,
    sunlit,
    coszen,
    albedo,
    ground_temp,
    aerosol,
    k_long,
    planck,
    k_short,
    solar_flux,
):
    fields, levels, columns = dyn_state.shape
    devices = lax.axis_size("gx") * lax.axis_size("gy")
    me = lax.axis_index(AXES).astype(jnp.int32).reshape(1)
    map_row = span_map.reshape(1, columns)
    swap = functools.partial(lax.all_to_all, axis_name=AXES, split_axis=0, concat_axis=0, tiled=True)

    outgoing, pick = pack(me, map_row, dyn_state, devices)
    width = outgoing.shape[1]
    recv = swap(outgoing.reshape(devices, 2 * CAP, width)).reshape(devices * 2 * CAP, width)
    fields_base, kept, coefficients, weights = base(
        me, map_row, dyn_state, aerosol, k_long, k_short, planck, solar_flux
    )
    row = lambda x: x.reshape(1, columns)
    heat, surface, back = flux(
        recv,
        fields_base,
        kept,
        coefficients,
        weights,
        row(coszen),
        row(albedo),
        row(ground_temp),
        row(sunlit),
        fields,
        planck.shape[0],
    )

    returned = swap(back.reshape(devices, 2, 128)).reshape(devices * 2, 128)
    whole = pl.BlockSpec(memory_space=pltpu.VMEM)
    local = pl.pallas_call(
        local_kernel,
        in_specs=[pl.BlockSpec(memory_space=pltpu.SMEM), whole, whole],
        out_specs=whole,
        out_shape=jax.ShapeDtypeStruct((levels, columns), F32),
        cost_estimate=pl.CostEstimate(
            flops=4 * levels * columns * columns, bytes_accessed=MIB, transcendentals=0
        ),
        name="local",
    )(me, map_row, heat)
    heating = pl.pallas_call(
        unpack_kernel,
        in_specs=[whole] * 3,
        out_specs=whole,
        out_shape=jax.ShapeDtypeStruct((levels, columns), F32),
        cost_estimate=pl.CostEstimate(
            flops=8 * levels * columns * columns, bytes_accessed=MIB, transcendentals=0
        ),
        name="unpack",
    )(local, pick, returned)
    return heating, surface


def solution(mesh):
    cols = P(AXES)
    in_specs = (
        P(None, None, AXES),
        cols,
        cols,
        cols,
        cols,
        cols,
        P(None, None, AXES),
        P(),
        P(),
        P(),
        P(),
    )
    out_specs = (P(None, AXES), P(None, AXES))
    return jax.shard_map(shards, mesh=mesh, in_specs=in_specs, out_specs=out_specs, check_vma=False)
```

```python
import functools

import jax
import jax.numpy as jnp
from jax import lax
from jax.experimental import pallas as pl
from jax.experimental.pallas import tpu as pltpu
from jax.sharding import PartitionSpec as P

AXES = ("gx", "gy")
DIFFUSE = 1.66
SCATTER = 0.3
SW_DEPTH = 2.0
LOG2E = 1.4426950408889634
CAP = 4
BF16 = jnp.bfloat16
F32 = jnp.float32
NT = (((1,), (1,)), ((), ()))
TN = (((0,), (0,)), ((), ()))
MIB = 1 << 20
HEAD, TAIL = 48, 64


def onehot(mask):
    return jnp.where(mask, 1.0, 0.0).astype(BF16)


def halves(x):
    high = x.astype(BF16)
    return high, (x - high.astype(F32)).astype(BF16)


def softplus2(u):
    return jnp.maximum(u, jnp.log2(1.0 + jnp.exp2(jnp.minimum(u, 126.0))))


def pack_kernel(me_ref, map_ref, dyn_ref, out_ref, pick_ref, place_ref, meta_ref):
    columns = map_ref.shape[1]
    rows = place_ref.shape[0]
    devices = rows // (2 * CAP)
    step = pl.program_id(0)
    last = pl.num_programs(0) - 1

    @pl.when(step == 0)
    def _():
        where_to = map_ref[...]
        target = where_to // columns
        slot = where_to % columns
        same = target == lax.broadcasted_iota(jnp.int32, (devices, columns), 0)
        earlier = onehot(
            lax.broadcasted_iota(jnp.int32, (columns, columns), 0)
            < lax.broadcasted_iota(jnp.int32, (columns, columns), 1)
        )
        before = jnp.dot(onehot(same), earlier, preferred_element_type=F32)
        rank = jnp.sum(jnp.where(same, before, 0.0), axis=0, keepdims=True).astype(jnp.int32)
        rank = jnp.where(target == me_ref[0], CAP, rank)
        for place in range(CAP):
            pick_ref[place * devices : (place + 1) * devices, :] = onehot(same & (rank == place))
        key = jnp.where(rank < CAP, (target * CAP + rank) * 2, 2 * rows)
        line = lax.broadcasted_iota(jnp.int32, (128, columns), 0)
        mark = slot + 1
        meta = jnp.where(line == 0, mark // 2, jnp.where(line == 1, mark % 2, 0)).astype(F32)
        for half in range(2):
            lanes = slice(half * columns, (half + 1) * columns)
            meta_ref[:, lanes] = meta.astype(BF16)
            for start in range(0, rows, 128):
                line = lax.broadcasted_iota(jnp.int32, (128, columns), 0) + start
                place_ref[start : start + 128, lanes] = onehot(line == key + half)

    @pl.when(step < last)
    def _():
        count = dyn_ref.shape[0] * 32
        both = [dyn_ref[:, half * 32 : half * 32 + 32, :].reshape(count, columns) for half in range(2)]
        out_ref[...] = lax.dot_general(
            place_ref[...], jnp.concatenate(both, axis=1), NT, preferred_element_type=F32
        ).astype(BF16)

    @pl.when(step == last)
    def _():
        out_ref[:, :128] = lax.dot_general(
            place_ref[...], meta_ref[...], NT, preferred_element_type=F32
        ).astype(BF16)


def pack(me, map_row, dyn_state, devices):
    fields, levels, columns = dyn_state.shape
    steps = fields // 8
    rows = devices * CAP * 2
    return pl.pallas_call(
        pack_kernel,
        grid=(steps + 1,),
        in_specs=[
            pl.BlockSpec(memory_space=pltpu.SMEM),
            pl.BlockSpec((1, columns), lambda i: (0, 0)),
            pl.BlockSpec((8, levels, columns), lambda i: (jnp.minimum(i, steps - 1), 0, 0)),
        ],
        out_specs=[
            pl.BlockSpec((rows, 256), lambda i: (0, i)),
            pl.BlockSpec((devices * CAP, columns), lambda i: (0, 0)),
        ],
        out_shape=[
            jax.ShapeDtypeStruct((rows, steps * 256 + 128), BF16),
            jax.ShapeDtypeStruct((devices * CAP, columns), BF16),
        ],
        scratch_shapes=[
            pltpu.VMEM((rows, 2 * columns), BF16),
            pltpu.VMEM((128, 2 * columns), BF16),
        ],
        compiler_params=pltpu.CompilerParams(vmem_limit_bytes=56 * MIB),
        cost_estimate=pl.CostEstimate(
            flops=4 * fields * levels * columns * devices * CAP, bytes_accessed=6 * MIB, transcendentals=0
        ),
        name="pack",
    )(me, map_row, dyn_state)


def base_kernel(
    me_ref,
    map_ref,
    dyn_ref,
    aer_ref,
    long_ref,
    short_ref,
    planck_ref,
    solar_ref,
    aero_ref,
    kept_ref,
    k_ref,
    weight_ref,
    pick_ref,
    rows_ref,
    wide_ref,
):
    fields, depth, columns = dyn_ref.shape
    extra = aer_ref.shape[0]
    tiles = columns // 128
    glw, gsw = long_ref.shape[0], short_ref.shape[0]

    @pl.when(pl.program_id(0) == 0)
    def _():
        goal = lax.broadcasted_iota(jnp.int32, (columns, columns), 0) + me_ref[0] * columns
        pick_ref[...] = onehot(map_ref[...] == goal)
        wide_ref[...] = jnp.zeros(wide_ref.shape, F32)
        for coefficients, start in ((long_ref[...], 0), (short_ref[...], glw)):
            scaled = coefficients.astype(F32) * LOG2E
            rows = slice(start, start + coefficients.shape[0])
            for first, part in zip((0, HEAD + TAIL), halves(scaled)):
                part = part.astype(F32)
                wide_ref[rows, first : first + fields] = part[:, :fields]
                wide_ref[rows, first + HEAD : first + HEAD + extra] = part[:, fields:]
        k_ref[...] = wide_ref[...].astype(BF16)
        square = lax.broadcasted_iota(jnp.int32, (128, 128), 0) == lax.broadcasted_iota(
            jnp.int32, (128, 128), 1
        )
        for source, start in ((planck_ref[...], 0), (solar_ref[...], glw)):
            size = source.shape[1]
            picked = jnp.where(square[:size, :size], source, 0.0)
            weight_ref[start : start + size, :] = jnp.broadcast_to(
                jnp.sum(picked, axis=1, keepdims=True), (size, 128)
            )

    kept = lax.dot_general(
        dyn_ref[...].reshape(fields * depth, columns), pick_ref[...], NT, preferred_element_type=F32
    )
    kept_ref[0] = kept.astype(BF16).reshape(fields, depth, columns)
    more = aer_ref[...].reshape(extra * depth, columns).astype(F32)
    for tile in range(tiles):
        rows_ref[tile] = more[:, tile * 128 : tile * 128 + 128]
    for tile in range(tiles):
        for level in range(depth):
            aero = rows_ref[tile, pl.ds(level, extra, stride=depth), :]
            aero_ref[tile, level] = jnp.concatenate(
                [aero, jnp.zeros((TAIL - extra, 128), F32)], axis=0
            ).astype(BF16)


def base(me, map_row, dyn_state, aerosol, k_long, k_short, planck, solar):
    fields, levels, columns = dyn_state.shape
    extra = aerosol.shape[0]
    glw, gsw = k_long.shape[0], k_short.shape[0]
    depth = 16
    tiles = columns // 128
    fixed = lambda *shape: pl.BlockSpec(shape, lambda i: (0,) * len(shape))
    return pl.pallas_call(
        base_kernel,
        grid=(levels // depth,),
        in_specs=[
            pl.BlockSpec(memory_space=pltpu.SMEM),
            fixed(1, columns),
            pl.BlockSpec((fields, depth, columns), lambda i: (0, i, 0)),
            pl.BlockSpec((extra, depth, columns), lambda i: (0, i, 0)),
            fixed(*k_long.shape),
            fixed(*k_short.shape),
            fixed(1, glw),
            fixed(1, gsw),
        ],
        out_specs=[
            pl.BlockSpec((tiles, depth, TAIL, 128), lambda i: (0, i, 0, 0)),
            pl.BlockSpec((1, fields, depth, columns), lambda i: (i // 2, 0, i % 2, 0)),
            fixed(glw + gsw, 2 * (HEAD + TAIL)),
            fixed(glw + gsw, 128),
        ],
        out_shape=[
            jax.ShapeDtypeStruct((tiles, levels, TAIL, 128), BF16),
            jax.ShapeDtypeStruct((2, fields, levels // 2, columns), BF16),
            jax.ShapeDtypeStruct((glw + gsw, 2 * (HEAD + TAIL)), BF16),
            jax.ShapeDtypeStruct((glw + gsw, 128), F32),
        ],
        scratch_shapes=[
            pltpu.VMEM((columns, columns), BF16),
            pltpu.VMEM((tiles, extra * depth, 128), F32),
            pltpu.VMEM((glw + gsw, 2 * (HEAD + TAIL)), F32),
        ],
        compiler_params=pltpu.CompilerParams(vmem_limit_bytes=56 * MIB),
        cost_estimate=pl.CostEstimate(
            flops=2 * fields * levels * columns * columns, bytes_accessed=14 * MIB, transcendentals=0
        ),
        name="base",
    )(me, map_row, dyn_state, aerosol, k_long, k_short, planck.reshape(1, glw), solar.reshape(1, gsw))


def flux_kernel(
    recv_hbm,
    aero_hbm,
    kept_hbm,
    k_ref,
    weight_ref,
    cos_ref,
    albedo_ref,
    ground_ref,
    lit_ref,
    heat_ref,
    surface_ref,
    back_ref,
    recv_ref,
    aero_ref,
    kept_ref,
    pick_ref,
    state_ref,
    delta_ref,
    trans_refs,
    down_refs,
    scat_refs,
    diff_refs,
    depth_refs,
    up_ref,
    beam_ref,
    spread_ref,
    return_ref,
    net_lw_ref,
    net_sw_ref,
    sems,
):
    rows = recv_ref.shape[0]
    devices = rows // (2 * CAP)
    tiles, levels, _, _ = aero_ref.shape
    columns = 128 * tiles
    glw, gsw = up_ref.shape[0], return_ref.shape[0]
    tall = state_ref.shape[1]
    fields = tall // 32
    pairs = levels // 2

    copies = [
        pltpu.make_async_copy(source, target, sems.at[i])
        for i, (source, target) in enumerate(
            [(recv_hbm, recv_ref), (kept_hbm, kept_ref)]
            + [(aero_hbm.at[tile], aero_ref.at[tile]) for tile in range(tiles)]
        )
    ]
    for copy in copies:
        copy.start()

    lanes_of = lambda tile: slice(tile * 128, tile * 128 + 128)
    copies[0].wait()
    mark = recv_ref[:, tall : tall + 128].astype(F32)
    mark = (mark[:, 0:1] * 2.0 + mark[:, 1:2]).astype(jnp.int32)
    half_of = lax.broadcasted_iota(jnp.int32, (rows, 1), 0) % 2
    for half in range(2):
        key = jnp.where(half_of == half, mark, 0)
        for tile in range(0, columns, 128):
            lane = lax.broadcasted_iota(jnp.int32, (rows, 128), 1) + (tile + 1)
            pick_ref[:, half * columns + tile : half * columns + tile + 128] = onehot(key == lane)
    copies[1].wait()
    for tile in range(0, tall, 128):
        moved = lax.dot_general(
            recv_ref[:, tile : tile + 128], pick_ref[...], TN, preferred_element_type=F32
        )
        for part in range(2 * tiles):
            stayed = kept_ref[part // tiles, tile // 32 : tile // 32 + 4, :, lanes_of(part % tiles)]
            state_ref[part, tile : tile + 128, :] = moved[:, lanes_of(part)] + stayed.reshape(
                128, 128
            ).astype(F32)

    for tile in range(tiles):
        cold = jnp.concatenate([state_ref[tile, :32, :], state_ref[tiles + tile, :32, :]], axis=0)
        warmth = softplus2(cold * LOG2E) * (1.0 / LOG2E)
        step = warmth - jnp.concatenate([warmth[1:], jnp.zeros((1, 128), F32)], axis=0)
        delta_ref[0, :, lanes_of(tile)] = jnp.broadcast_to(warmth[0:1], (8, 128))
        for level in range(levels):
            delta_ref[level + 1, :, lanes_of(tile)] = jnp.broadcast_to(step[level : level + 1], (8, 128))

    cosine, albedo, ground = cos_ref[...], albedo_ref[...], ground_ref[...]
    lit = lit_ref[...].astype(F32)
    slant = (-SW_DEPTH / levels) / cosine
    skin = softplus2(ground * LOG2E) * (1.0 / LOG2E)

    def absorb(pair, tile):
        half = pair // (pairs // 2)
        inner = 2 * pair - 32 * half
        both = [
            state_ref[half * tiles + tile, pl.ds(inner + e, fields, stride=32), :] for e in range(2)
        ]
        here = jnp.concatenate(
            [jnp.concatenate(both, axis=1), jnp.zeros((HEAD - fields, 256), F32)], axis=0
        ).astype(BF16)
        rest = jnp.concatenate([aero_ref[tile, 2 * pair + e] for e in range(2)], axis=1)
        return jnp.dot(
            k_ref[...], jnp.concatenate([here, rest, here, rest], axis=0), preferred_element_type=F32
        )

    def both_ways(pair, tile, depth_ref, following, following_tile, following_ref):
        descends, ascends = tile < tiles, tile > 0
        if descends:
            following_ref[...] = absorb(following, following_tile)
            trans_ref, down_ref = trans_refs[tile % 2], down_refs[tile % 2]
            scat_ref, diff_ref = scat_refs[tile % 2], diff_refs[tile % 2]
            level = 2 * pair
            lanes = lanes_of(tile)
            delta = [delta_ref[level + e + 1, :, lanes] for e in range(2)]
            slope = jnp.broadcast_to(slant[:, lanes], (8, 128))
            sum_beam = [jnp.zeros((8, 128), F32) for _ in range(2)]
            sum_spread = [jnp.zeros((8, 128), F32) for _ in range(2)]
        if ascends:
            old_trans, old_down = trans_refs[1 - tile % 2], down_refs[1 - tile % 2]
            old_scat, old_diff = scat_refs[1 - tile % 2], diff_refs[1 - tile % 2]
            old_level = 2 * (pairs - 1 - pair)
            old_lanes = lanes_of(tile - 1)
            old_delta = [delta_ref[old_level + e, :, old_lanes] for e in range(2)]
            total_lw = [jnp.zeros((8, 128), F32) for _ in range(2)]
            total_sw = [net_sw_ref[old_level + e, :, old_lanes] for e in range(2)]

        for g in range(0, glw, 8):
            if descends:
                down = down_ref[level, g : g + 8, :]
                for e in range(2):
                    u = depth_ref[g : g + 8, 128 * e : 128 * e + 128]
                    tau = jnp.log2(1.0 + jnp.exp2(jnp.minimum(u, 126.0)))
                    trans = jnp.exp2(tau * (-DIFFUSE))
                    trans_ref[level + e, g : g + 8, :] = trans
                    down = trans * down + delta[e]
                    down_ref[level + e + 1, g : g + 8, :] = down
            if ascends:
                upper = up_ref[g : g + 8, :]
                weight = weight_ref[g : g + 8, :]
                for e in (1, 0):
                    passed = old_trans[old_level + e, g : g + 8, :] * upper
                    total_lw[e] = total_lw[e] + weight * (old_down[old_level + e, g : g + 8, :] - passed)
                    upper = passed - old_delta[e]
                up_ref[g : g + 8, :] = upper
        for g in range(0, gsw, 8):
            if descends:
                beam = beam_ref[g : g + 8, :]
                spread = spread_ref[g : g + 8, :]
                for e in range(2):
                    u = depth_ref[glw + g : glw + g + 8, 128 * e : 128 * e + 128]
                    tau = jnp.maximum(u, jnp.log2(1.0 + jnp.exp2(jnp.minimum(u, 126.0))))
                    diffuse = jnp.exp2(tau * (-DIFFUSE * SW_DEPTH / levels))
                    diff_ref[level + e, g : g + 8, :] = diffuse
                    lower = jnp.exp2(tau * slope) * beam
                    scattered = beam - lower
                    scat_ref[level + e, g : g + 8, :] = scattered
                    sum_beam[e] = sum_beam[e] + beam
                    sum_spread[e] = sum_spread[e] + spread
                    spread = diffuse * spread + scattered
                    beam = lower
                beam_ref[g : g + 8, :] = beam
                spread_ref[g : g + 8, :] = spread
            if ascends:
                upper = return_ref[g : g + 8, :]
                for e in (1, 0):
                    upper = (
                        old_diff[old_level + e, g : g + 8, :] * upper
                        + old_scat[old_level + e, g : g + 8, :]
                    )
                    total_sw[e] = total_sw[e] - upper
                return_ref[g : g + 8, :] = upper
        for e in range(2):
            if descends:
                net_sw_ref[level + e, :, lanes] = sum_beam[e] * (1.0 / SCATTER) + sum_spread[e]
            if ascends:
                net_lw_ref[old_level + e, :, old_lanes] = total_lw[e]
                net_sw_ref[old_level + e, :, old_lanes] = total_sw[e]

    def turn(tile):
        lanes = lanes_of(tile)
        down_ref = down_refs[tile % 2]
        total = jnp.zeros((8, 128), F32)
        floor_total = jnp.zeros((8, 128), F32)
        upper = jnp.broadcast_to(skin[:, lanes], (8, 128))
        above = upper - delta_ref[levels, :, lanes]
        for g in range(0, glw, 8):
            weight = weight_ref[g : g + 8, :]
            floor = weight * down_ref[levels, g : g + 8, :]
            floor_total = floor_total + floor
            total = total + (floor - weight * upper)
            up_ref[g : g + 8, :] = above
        net_lw_ref[levels, :, lanes] = total
        surface_ref[0:1, lanes] = jnp.sum(floor_total, axis=0, keepdims=True) * (1.0 / glw)
        bright = jnp.broadcast_to(albedo[:, lanes], (8, 128))
        floor_total = jnp.zeros((8, 128), F32)
        for g in range(0, gsw, 8):
            floor = beam_ref[g : g + 8, :] * (1.0 / SCATTER) + spread_ref[g : g + 8, :]
            floor_total = floor_total + floor
            return_ref[g : g + 8, :] = bright * floor
        net_sw_ref[levels, :, lanes] = floor_total - bright * floor_total
        surface_ref[1:2, lanes] = jnp.sum(floor_total, axis=0, keepdims=True) * (
            lit[:, lanes] * cosine[:, lanes] * (1.0 / gsw)
        )

    copies[2].wait()
    depth_refs[0][...] = absorb(0, 0)
    for tile in range(tiles + 1):
        if tile + 1 < tiles:
            copies[2 + tile + 1].wait()
        if tile < tiles:
            first = 0.0 - delta_ref[0, :, lanes_of(tile)]
            for g in range(0, glw, 8):
                down_refs[tile % 2][0, g : g + 8, :] = first
            spread_ref[...] = jnp.zeros((gsw, 128), F32)
            beam_ref[...] = SCATTER * weight_ref[glw:, :]

        def two_pairs(step, _, tile=tile):
            for part in range(2):
                pair = 2 * step + part
                over = pair == pairs - 1
                following = jnp.where(over, 0, pair + 1)
                following_tile = jnp.where(over, min(tile + 1, tiles - 1), tile)
                both_ways(
                    pair, tile, depth_refs[part], following, following_tile, depth_refs[1 - part]
                )
            return 0

        lax.fori_loop(0, pairs // 2, two_pairs, 0, unroll=4)
        if tile < tiles:
            turn(tile)

    net_lw = jnp.sum(net_lw_ref[...], axis=1)
    net_sw = jnp.sum(net_sw_ref[...], axis=1)
    heat = (net_lw[:levels] - net_lw[1 : levels + 1]) * (1.0 / glw) + (
        net_sw[:levels] - net_sw[1 : levels + 1]
    ) * (lit * cosine * (1.0 / gsw))
    heat_ref[...] = heat

    twice = jnp.concatenate([heat, heat], axis=0)
    high, low = halves(twice)
    picked = pick_ref[:, :columns]
    state_ref[0, :rows, :] = lax.dot_general(picked, high, NT, preferred_element_type=F32) + lax.dot_general(
        picked, low, NT, preferred_element_type=F32
    )
    left = lax.broadcasted_iota(jnp.int32, (devices, 128), 1) < levels
    for pair in range(2):
        even = state_ref[0, pl.ds(4 * pair, devices, stride=8), :]
        odd = state_ref[0, pl.ds(4 * pair + 2, devices, stride=8), :]
        back_ref[pl.ds(pair, devices, stride=2), :] = jnp.where(left, even, odd)


def flux(recv, aero, kept, coefficients, weights, coszen, albedo, ground, sunlit, fields, glw):
    rows, width = recv.shape
    tiles, levels, _, _ = aero.shape
    columns = 128 * tiles
    gsw = weights.shape[0] - glw
    devices = rows // (2 * CAP)
    whole = pl.BlockSpec(memory_space=pltpu.VMEM)
    count = (glw + gsw) * levels * columns
    twice = lambda *shape: [pltpu.VMEM(shape, F32)] * 2
    return pl.pallas_call(
        flux_kernel,
        in_specs=[pl.BlockSpec(memory_space=pl.ANY)] * 3 + [whole] * 6,
        out_specs=[whole] * 3,
        out_shape=[
            jax.ShapeDtypeStruct((levels, columns), F32),
            jax.ShapeDtypeStruct((2, columns), F32),
            jax.ShapeDtypeStruct((devices * 2, 128), F32),
        ],
        scratch_shapes=[
            pltpu.VMEM((rows, width), BF16),
            pltpu.VMEM(aero.shape, BF16),
            pltpu.VMEM(kept.shape, BF16),
            pltpu.VMEM((rows, 2 * columns), BF16),
            pltpu.VMEM((2 * tiles, fields * 32, 128), F32),
            pltpu.VMEM((levels + 1, 8, columns), F32),
            twice(levels, glw, 128),
            twice(levels + 1, glw, 128),
            twice(levels, gsw, 128),
            twice(levels, gsw, 128),
            twice(glw + gsw, 256),
            pltpu.VMEM((glw, 128), F32),
            pltpu.VMEM((gsw, 128), F32),
            pltpu.VMEM((gsw, 128), F32),
            pltpu.VMEM((gsw, 128), F32),
            pltpu.VMEM((levels + 1, 8, columns), F32),
            pltpu.VMEM((levels + 1, 8, columns), F32),
            pltpu.SemaphoreType.DMA((2 + tiles,)),
        ],
        compiler_params=pltpu.CompilerParams(vmem_limit_bytes=54 * MIB),
        cost_estimate=pl.CostEstimate(flops=250 * count, bytes_accessed=12 * MIB, transcendentals=4 * count),
        name="flux",
    )(recv, aero, kept, coefficients, weights, coszen, albedo, ground, sunlit)


def local_kernel(me_ref, map_ref, heat_ref, out_ref):
    columns = map_ref.shape[1]
    goal = lax.broadcasted_iota(jnp.int32, (columns, columns), 0) + me_ref[0] * columns
    stay = onehot(map_ref[...] == goal)
    high, low = halves(heat_ref[...])
    out_ref[...] = jnp.dot(high, stay, preferred_element_type=F32) + jnp.dot(
        low, stay, preferred_element_type=F32
    )


def unpack_kernel(local_ref, pick_ref, back_ref, out_ref):
    devices = back_ref.shape[0] // 2
    levels = local_ref.shape[0]
    total = local_ref[...]
    for pair in range(2):
        high, low = halves(back_ref[pl.ds(pair, devices, stride=2), :])
        for side in range(2):
            place = 2 * pair + side
            pick = pick_ref[place * devices : (place + 1) * devices, :]
            part = lax.dot_general(high, pick, TN, preferred_element_type=F32) + lax.dot_general(
                low, pick, TN, preferred_element_type=F32
            )
            total = total + part[side * levels : (side + 1) * levels]
    out_ref[...] = total


def shards(
    dyn_state,
    span_map,
    sunlit,
    coszen,
    albedo,
    ground_temp,
    aerosol,
    k_long,
    planck,
    k_short,
    solar_flux,
):
    fields, levels, columns = dyn_state.shape
    devices = lax.axis_size("gx") * lax.axis_size("gy")
    me = lax.axis_index(AXES).astype(jnp.int32).reshape(1)
    map_row = span_map.reshape(1, columns)
    swap = functools.partial(lax.all_to_all, axis_name=AXES, split_axis=0, concat_axis=0, tiled=True)

    outgoing, pick = pack(me, map_row, dyn_state, devices)
    width = outgoing.shape[1]
    recv = swap(outgoing.reshape(devices, 2 * CAP, width)).reshape(devices * 2 * CAP, width)
    aero, kept, coefficients, weights = base(
        me, map_row, dyn_state, aerosol, k_long, k_short, planck, solar_flux
    )
    row = lambda x: x.reshape(1, columns)
    heat, surface, back = flux(
        recv,
        aero,
        kept,
        coefficients,
        weights,
        row(coszen),
        row(albedo),
        row(ground_temp),
        row(sunlit),
        fields,
        planck.shape[0],
    )

    returned = swap(back.reshape(devices, 2, 128)).reshape(devices * 2, 128)
    whole = pl.BlockSpec(memory_space=pltpu.VMEM)
    local = pl.pallas_call(
        local_kernel,
        in_specs=[pl.BlockSpec(memory_space=pltpu.SMEM), whole, whole],
        out_specs=whole,
        out_shape=jax.ShapeDtypeStruct((levels, columns), F32),
        cost_estimate=pl.CostEstimate(
            flops=4 * levels * columns * columns, bytes_accessed=MIB, transcendentals=0
        ),
        name="local",
    )(me, map_row, heat)
    heating = pl.pallas_call(
        unpack_kernel,
        in_specs=[whole] * 3,
        out_specs=whole,
        out_shape=jax.ShapeDtypeStruct((levels, columns), F32),
        cost_estimate=pl.CostEstimate(
            flops=8 * levels * columns * columns, bytes_accessed=MIB, transcendentals=0
        ),
        name="unpack",
    )(local, pick, returned)
    return heating, surface


def solution(mesh):
    cols = P(AXES)
    in_specs = (
        P(None, None, AXES),
        cols,
        cols,
        cols,
        cols,
        cols,
        P(None, None, AXES),
        P(),
        P(),
        P(),
        P(),
    )
    out_specs = (P(None, AXES), P(None, AXES))
    return jax.shard_map(shards, mesh=mesh, in_specs=in_specs, out_specs=out_specs, check_vma=False)
```

```python
import functools

import jax
import jax.numpy as jnp
from jax import lax
from jax.experimental import pallas as pl
from jax.experimental.pallas import tpu as pltpu
from jax.sharding import PartitionSpec as P

AXES = ("gx", "gy")
DIFFUSE = 1.66
SCATTER = 0.3
SW_DEPTH = 2.0
LOG2E = 1.4426950408889634
CAP = 4
BF16 = jnp.bfloat16
F32 = jnp.float32
NT = (((1,), (1,)), ((), ()))
TN = (((0,), (0,)), ((), ()))
MIB = 1 << 20
HEAD, TAIL = 48, 64


def onehot(mask):
    return jnp.where(mask, 1.0, 0.0).astype(BF16)


def halves(x):
    high = x.astype(BF16)
    return high, (x - high.astype(F32)).astype(BF16)


def softplus2(u):
    return jnp.maximum(u, jnp.log2(1.0 + jnp.exp2(jnp.minimum(u, 126.0))))


def pack_kernel(me_ref, map_ref, dyn_ref, out_ref, pick_ref, place_ref, meta_ref):
    columns = map_ref.shape[1]
    rows = place_ref.shape[0]
    devices = rows // (2 * CAP)
    step = pl.program_id(0)
    last = pl.num_programs(0) - 1

    @pl.when(step == 0)
    def _():
        where_to = map_ref[...]
        target = where_to // columns
        slot = where_to % columns
        same = target == lax.broadcasted_iota(jnp.int32, (devices, columns), 0)
        earlier = onehot(
            lax.broadcasted_iota(jnp.int32, (columns, columns), 0)
            < lax.broadcasted_iota(jnp.int32, (columns, columns), 1)
        )
        before = jnp.dot(onehot(same), earlier, preferred_element_type=F32)
        rank = jnp.sum(jnp.where(same, before, 0.0), axis=0, keepdims=True).astype(jnp.int32)
        rank = jnp.where(target == me_ref[0], CAP, rank)
        for place in range(CAP):
            pick_ref[place * devices : (place + 1) * devices, :] = onehot(same & (rank == place))
        key = jnp.where(rank < CAP, (target * CAP + rank) * 2, 2 * rows)
        line = lax.broadcasted_iota(jnp.int32, (128, columns), 0)
        mark = slot + 1
        meta = jnp.where(line == 0, mark // 2, jnp.where(line == 1, mark % 2, 0)).astype(F32)
        for half in range(2):
            lanes = slice(half * columns, (half + 1) * columns)
            meta_ref[:, lanes] = meta.astype(BF16)
            for start in range(0, rows, 128):
                line = lax.broadcasted_iota(jnp.int32, (128, columns), 0) + start
                place_ref[start : start + 128, lanes] = onehot(line == key + half)

    @pl.when(step < last)
    def _():
        count = dyn_ref.shape[0] * 32
        both = [dyn_ref[:, half * 32 : half * 32 + 32, :].reshape(count, columns) for half in range(2)]
        out_ref[...] = lax.dot_general(
            place_ref[...], jnp.concatenate(both, axis=1), NT, preferred_element_type=F32
        ).astype(BF16)

    @pl.when(step == last)
    def _():
        out_ref[:, :128] = lax.dot_general(
            place_ref[...], meta_ref[...], NT, preferred_element_type=F32
        ).astype(BF16)


def pack(me, map_row, dyn_state, devices):
    fields, levels, columns = dyn_state.shape
    steps = 1
    rows = devices * CAP * 2
    return pl.pallas_call(
        pack_kernel,
        grid=(steps + 1,),
        in_specs=[
            pl.BlockSpec(memory_space=pltpu.SMEM),
            pl.BlockSpec((1, columns), lambda i: (0, 0)),
            pl.BlockSpec((fields, levels, columns), lambda i: (jnp.minimum(i, steps - 1), 0, 0)),
        ],
        out_specs=[
            pl.BlockSpec((rows, fields * 32), lambda i: (0, i)),
            pl.BlockSpec((devices * CAP, columns), lambda i: (0, 0)),
        ],
        out_shape=[
            jax.ShapeDtypeStruct((rows, fields * 32 + 128), BF16),
            jax.ShapeDtypeStruct((devices * CAP, columns), BF16),
        ],
        scratch_shapes=[
            pltpu.VMEM((rows, 2 * columns), BF16),
            pltpu.VMEM((128, 2 * columns), BF16),
        ],
        compiler_params=pltpu.CompilerParams(vmem_limit_bytes=56 * MIB),
        cost_estimate=pl.CostEstimate(
            flops=4 * fields * levels * columns * devices * CAP, bytes_accessed=6 * MIB, transcendentals=0
        ),
        name="pack",
    )(me, map_row, dyn_state)


def base_kernel(
    me_ref,
    map_ref,
    dyn_ref,
    aer_ref,
    long_ref,
    short_ref,
    planck_ref,
    solar_ref,
    aero_ref,
    kept_ref,
    k_ref,
    weight_ref,
    pick_ref,
    rows_ref,
    wide_ref,
):
    fields, depth, columns = dyn_ref.shape
    extra = aer_ref.shape[0]
    tiles = columns // 128
    glw, gsw = long_ref.shape[0], short_ref.shape[0]

    @pl.when(pl.program_id(0) == 0)
    def _():
        goal = lax.broadcasted_iota(jnp.int32, (columns, columns), 0) + me_ref[0] * columns
        pick_ref[...] = onehot(map_ref[...] == goal)
        wide_ref[...] = jnp.zeros(wide_ref.shape, F32)
        for coefficients, start in ((long_ref[...], 0), (short_ref[...], glw)):
            scaled = coefficients.astype(F32) * LOG2E
            rows = slice(start, start + coefficients.shape[0])
            for first, part in zip((0, HEAD + TAIL), halves(scaled)):
                part = part.astype(F32)
                wide_ref[rows, first : first + fields] = part[:, :fields]
                wide_ref[rows, first + HEAD : first + HEAD + extra] = part[:, fields:]
        k_ref[...] = wide_ref[...].astype(BF16)
        square = lax.broadcasted_iota(jnp.int32, (128, 128), 0) == lax.broadcasted_iota(
            jnp.int32, (128, 128), 1
        )
        for source, start in ((planck_ref[...], 0), (solar_ref[...], glw)):
            size = source.shape[1]
            picked = jnp.where(square[:size, :size], source, 0.0)
            weight_ref[start : start + size, :] = jnp.broadcast_to(
                jnp.sum(picked, axis=1, keepdims=True), (size, 128)
            )

    kept = lax.dot_general(
        dyn_ref[...].reshape(fields * depth, columns), pick_ref[...], NT, preferred_element_type=F32
    )
    kept_ref[0] = kept.astype(BF16).reshape(fields, depth, columns)
    more = aer_ref[...].reshape(extra * depth, columns).astype(F32)
    for tile in range(tiles):
        rows_ref[tile] = more[:, tile * 128 : tile * 128 + 128]
    for tile in range(tiles):
        for level in range(depth):
            aero = rows_ref[tile, pl.ds(level, extra, stride=depth), :]
            aero_ref[tile, level] = jnp.concatenate(
                [aero, jnp.zeros((TAIL - extra, 128), F32)], axis=0
            ).astype(BF16)


def base(me, map_row, dyn_state, aerosol, k_long, k_short, planck, solar):
    fields, levels, columns = dyn_state.shape
    extra = aerosol.shape[0]
    glw, gsw = k_long.shape[0], k_short.shape[0]
    depth = 16
    tiles = columns // 128
    fixed = lambda *shape: pl.BlockSpec(shape, lambda i: (0,) * len(shape))
    return pl.pallas_call(
        base_kernel,
        grid=(levels // depth,),
        in_specs=[
            pl.BlockSpec(memory_space=pltpu.SMEM),
            fixed(1, columns),
            pl.BlockSpec((fields, depth, columns), lambda i: (0, i, 0)),
            pl.BlockSpec((extra, depth, columns), lambda i: (0, i, 0)),
            fixed(*k_long.shape),
            fixed(*k_short.shape),
            fixed(1, glw),
            fixed(1, gsw),
        ],
        out_specs=[
            pl.BlockSpec((tiles, depth, TAIL, 128), lambda i: (0, i, 0, 0)),
            pl.BlockSpec((1, fields, depth, columns), lambda i: (i // 2, 0, i % 2, 0)),
            fixed(glw + gsw, 2 * (HEAD + TAIL)),
            fixed(glw + gsw, 128),
        ],
        out_shape=[
            jax.ShapeDtypeStruct((tiles, levels, TAIL, 128), BF16),
            jax.ShapeDtypeStruct((2, fields, levels // 2, columns), BF16),
            jax.ShapeDtypeStruct((glw + gsw, 2 * (HEAD + TAIL)), BF16),
            jax.ShapeDtypeStruct((glw + gsw, 128), F32),
        ],
        scratch_shapes=[
            pltpu.VMEM((columns, columns), BF16),
            pltpu.VMEM((tiles, extra * depth, 128), F32),
            pltpu.VMEM((glw + gsw, 2 * (HEAD + TAIL)), F32),
        ],
        compiler_params=pltpu.CompilerParams(vmem_limit_bytes=56 * MIB),
        cost_estimate=pl.CostEstimate(
            flops=2 * fields * levels * columns * columns, bytes_accessed=14 * MIB, transcendentals=0
        ),
        name="base",
    )(me, map_row, dyn_state, aerosol, k_long, k_short, planck.reshape(1, glw), solar.reshape(1, gsw))


def flux_kernel(
    recv_hbm,
    aero_hbm,
    kept_hbm,
    k_ref,
    weight_ref,
    cos_ref,
    albedo_ref,
    ground_ref,
    lit_ref,
    heat_ref,
    surface_ref,
    back_ref,
    recv_ref,
    aero_ref,
    kept_ref,
    pick_ref,
    state_ref,
    delta_ref,
    trans_refs,
    down_refs,
    scat_refs,
    diff_refs,
    depth_refs,
    up_ref,
    beam_ref,
    spread_ref,
    return_ref,
    net_lw_ref,
    net_sw_ref,
    sems,
):
    rows = recv_ref.shape[0]
    devices = rows // (2 * CAP)
    tiles, levels, _, _ = aero_ref.shape
    columns = 128 * tiles
    glw, gsw = up_ref.shape[0], return_ref.shape[0]
    tall = state_ref.shape[1]
    fields = tall // 32
    pairs = levels // 2

    copies = [
        pltpu.make_async_copy(source, target, sems.at[i])
        for i, (source, target) in enumerate(
            [(recv_hbm, recv_ref), (kept_hbm, kept_ref)]
            + [(aero_hbm.at[tile], aero_ref.at[tile]) for tile in range(tiles)]
        )
    ]
    for copy in copies:
        copy.start()

    lanes_of = lambda tile: slice(tile * 128, tile * 128 + 128)
    copies[0].wait()
    mark = recv_ref[:, tall : tall + 128].astype(F32)
    mark = (mark[:, 0:1] * 2.0 + mark[:, 1:2]).astype(jnp.int32)
    half_of = lax.broadcasted_iota(jnp.int32, (rows, 1), 0) % 2
    for half in range(2):
        key = jnp.where(half_of == half, mark, 0)
        for tile in range(0, columns, 128):
            lane = lax.broadcasted_iota(jnp.int32, (rows, 128), 1) + (tile + 1)
            pick_ref[:, half * columns + tile : half * columns + tile + 128] = onehot(key == lane)
    copies[1].wait()
    for tile in range(0, tall, 128):
        moved = lax.dot_general(
            recv_ref[:, tile : tile + 128], pick_ref[...], TN, preferred_element_type=F32
        )
        for part in range(2 * tiles):
            stayed = kept_ref[part // tiles, tile // 32 : tile // 32 + 4, :, lanes_of(part % tiles)]
            state_ref[part, tile : tile + 128, :] = moved[:, lanes_of(part)] + stayed.reshape(
                128, 128
            ).astype(F32)

    for tile in range(tiles):
        cold = jnp.concatenate([state_ref[tile, :32, :], state_ref[tiles + tile, :32, :]], axis=0)
        warmth = softplus2(cold * LOG2E) * (1.0 / LOG2E)
        step = warmth - jnp.concatenate([warmth[1:], jnp.zeros((1, 128), F32)], axis=0)
        delta_ref[0, :, lanes_of(tile)] = jnp.broadcast_to(warmth[0:1], (8, 128))
        for level in range(levels):
            delta_ref[level + 1, :, lanes_of(tile)] = jnp.broadcast_to(step[level : level + 1], (8, 128))

    cosine, albedo, ground = cos_ref[...], albedo_ref[...], ground_ref[...]
    lit = lit_ref[...].astype(F32)
    slant = (-SW_DEPTH / levels) / cosine
    skin = softplus2(ground * LOG2E) * (1.0 / LOG2E)

    def absorb(pair, tile):
        half = pair // (pairs // 2)
        inner = 2 * pair - 32 * half
        both = [
            state_ref[half * tiles + tile, pl.ds(inner + e, fields, stride=32), :] for e in range(2)
        ]
        here = jnp.concatenate(
            [jnp.concatenate(both, axis=1), jnp.zeros((HEAD - fields, 256), F32)], axis=0
        ).astype(BF16)
        rest = jnp.concatenate([aero_ref[tile, 2 * pair + e] for e in range(2)], axis=1)
        return jnp.dot(
            k_ref[...], jnp.concatenate([here, rest, here, rest], axis=0), preferred_element_type=F32
        )

    def both_ways(pair, tile, depth_ref, following, following_tile, following_ref):
        descends, ascends = tile < tiles, tile > 0
        if descends:
            following_ref[...] = absorb(following, following_tile)
            trans_ref, down_ref = trans_refs[tile % 2], down_refs[tile % 2]
            scat_ref, diff_ref = scat_refs[tile % 2], diff_refs[tile % 2]
            level = 2 * pair
            lanes = lanes_of(tile)
            delta = [delta_ref[level + e + 1, :, lanes] for e in range(2)]
            slope = jnp.broadcast_to(slant[:, lanes], (8, 128))
            sum_beam = [jnp.zeros((8, 128), F32) for _ in range(2)]
            sum_spread = [jnp.zeros((8, 128), F32) for _ in range(2)]
        if ascends:
            old_trans, old_down = trans_refs[1 - tile % 2], down_refs[1 - tile % 2]
            old_scat, old_diff = scat_refs[1 - tile % 2], diff_refs[1 - tile % 2]
            old_level = 2 * (pairs - 1 - pair)
            old_lanes = lanes_of(tile - 1)
            old_delta = [delta_ref[old_level + e, :, old_lanes] for e in range(2)]
            total_lw = [jnp.zeros((8, 128), F32) for _ in range(2)]
            total_sw = [net_sw_ref[old_level + e, :, old_lanes] for e in range(2)]

        for g in range(0, glw, 8):
            if descends:
                down = down_ref[level, g : g + 8, :]
                for e in range(2):
                    u = depth_ref[g : g + 8, 128 * e : 128 * e + 128]
                    tau = jnp.log2(1.0 + jnp.exp2(jnp.minimum(u, 126.0)))
                    trans = jnp.exp2(tau * (-DIFFUSE))
                    trans_ref[level + e, g : g + 8, :] = trans
                    down = trans * down + delta[e]
                    down_ref[level + e + 1, g : g + 8, :] = down
            if ascends:
                upper = up_ref[g : g + 8, :]
                weight = weight_ref[g : g + 8, :]
                for e in (1, 0):
                    passed = old_trans[old_level + e, g : g + 8, :] * upper
                    total_lw[e] = total_lw[e] + weight * (old_down[old_level + e, g : g + 8, :] - passed)
                    upper = passed - old_delta[e]
                up_ref[g : g + 8, :] = upper
        for g in range(0, gsw, 8):
            if descends:
                beam = beam_ref[g : g + 8, :]
                spread = spread_ref[g : g + 8, :]
                for e in range(2):
                    u = depth_ref[glw + g : glw + g + 8, 128 * e : 128 * e + 128]
                    tau = jnp.maximum(u, jnp.log2(1.0 + jnp.exp2(jnp.minimum(u, 126.0))))
                    diffuse = jnp.exp2(tau * (-DIFFUSE * SW_DEPTH / levels))
                    diff_ref[level + e, g : g + 8, :] = diffuse
                    lower = jnp.exp2(tau * slope) * beam
                    scattered = beam - lower
                    scat_ref[level + e, g : g + 8, :] = scattered
                    sum_beam[e] = sum_beam[e] + beam
                    sum_spread[e] = sum_spread[e] + spread
                    spread = diffuse * spread + scattered
                    beam = lower
                beam_ref[g : g + 8, :] = beam
                spread_ref[g : g + 8, :] = spread
            if ascends:
                upper = return_ref[g : g + 8, :]
                for e in (1, 0):
                    upper = (
                        old_diff[old_level + e, g : g + 8, :] * upper
                        + old_scat[old_level + e, g : g + 8, :]
                    )
                    total_sw[e] = total_sw[e] - upper
                return_ref[g : g + 8, :] = upper
        for e in range(2):
            if descends:
                net_sw_ref[level + e, :, lanes] = sum_beam[e] * (1.0 / SCATTER) + sum_spread[e]
            if ascends:
                net_lw_ref[old_level + e, :, old_lanes] = total_lw[e]
                net_sw_ref[old_level + e, :, old_lanes] = total_sw[e]

    def turn(tile):
        lanes = lanes_of(tile)
        down_ref = down_refs[tile % 2]
        total = jnp.zeros((8, 128), F32)
        floor_total = jnp.zeros((8, 128), F32)
        upper = jnp.broadcast_to(skin[:, lanes], (8, 128))
        above = upper - delta_ref[levels, :, lanes]
        for g in range(0, glw, 8):
            weight = weight_ref[g : g + 8, :]
            floor = weight * down_ref[levels, g : g + 8, :]
            floor_total = floor_total + floor
            total = total + (floor - weight * upper)
            up_ref[g : g + 8, :] = above
        net_lw_ref[levels, :, lanes] = total
        surface_ref[0:1, lanes] = jnp.sum(floor_total, axis=0, keepdims=True) * (1.0 / glw)
        bright = jnp.broadcast_to(albedo[:, lanes], (8, 128))
        floor_total = jnp.zeros((8, 128), F32)
        for g in range(0, gsw, 8):
            floor = beam_ref[g : g + 8, :] * (1.0 / SCATTER) + spread_ref[g : g + 8, :]
            floor_total = floor_total + floor
            return_ref[g : g + 8, :] = bright * floor
        net_sw_ref[levels, :, lanes] = floor_total - bright * floor_total
        surface_ref[1:2, lanes] = jnp.sum(floor_total, axis=0, keepdims=True) * (
            lit[:, lanes] * cosine[:, lanes] * (1.0 / gsw)
        )

    copies[2].wait()
    depth_refs[0][...] = absorb(0, 0)
    for tile in range(tiles + 1):
        if tile + 1 < tiles:
            copies[2 + tile + 1].wait()
        if tile < tiles:
            first = 0.0 - delta_ref[0, :, lanes_of(tile)]
            for g in range(0, glw, 8):
                down_refs[tile % 2][0, g : g + 8, :] = first
            spread_ref[...] = jnp.zeros((gsw, 128), F32)
            beam_ref[...] = SCATTER * weight_ref[glw:, :]

        def two_pairs(step, _, tile=tile):
            for part in range(2):
                pair = 2 * step + part
                over = pair == pairs - 1
                following = jnp.where(over, 0, pair + 1)
                following_tile = jnp.where(over, min(tile + 1, tiles - 1), tile)
                both_ways(
                    pair, tile, depth_refs[part], following, following_tile, depth_refs[1 - part]
                )
            return 0

        lax.fori_loop(0, pairs // 2, two_pairs, 0, unroll=8)
        if tile < tiles:
            turn(tile)

    net_lw = jnp.sum(net_lw_ref[...], axis=1)
    net_sw = jnp.sum(net_sw_ref[...], axis=1)
    heat = (net_lw[:levels] - net_lw[1 : levels + 1]) * (1.0 / glw) + (
        net_sw[:levels] - net_sw[1 : levels + 1]
    ) * (lit * cosine * (1.0 / gsw))
    heat_ref[...] = heat

    twice = jnp.concatenate([heat, heat], axis=0)
    high, low = halves(twice)
    picked = pick_ref[:, :columns]
    state_ref[0, :rows, :] = lax.dot_general(picked, high, NT, preferred_element_type=F32) + lax.dot_general(
        picked, low, NT, preferred_element_type=F32
    )
    left = lax.broadcasted_iota(jnp.int32, (devices, 128), 1) < levels
    for pair in range(2):
        even = state_ref[0, pl.ds(4 * pair, devices, stride=8), :]
        odd = state_ref[0, pl.ds(4 * pair + 2, devices, stride=8), :]
        back_ref[pl.ds(pair, devices, stride=2), :] = jnp.where(left, even, odd)


def flux(recv, aero, kept, coefficients, weights, coszen, albedo, ground, sunlit, fields, glw):
    rows, width = recv.shape
    tiles, levels, _, _ = aero.shape
    columns = 128 * tiles
    gsw = weights.shape[0] - glw
    devices = rows // (2 * CAP)
    whole = pl.BlockSpec(memory_space=pltpu.VMEM)
    count = (glw + gsw) * levels * columns
    twice = lambda *shape: [pltpu.VMEM(shape, F32)] * 2
    return pl.pallas_call(
        flux_kernel,
        in_specs=[pl.BlockSpec(memory_space=pl.ANY)] * 3 + [whole] * 6,
        out_specs=[whole] * 3,
        out_shape=[
            jax.ShapeDtypeStruct((levels, columns), F32),
            jax.ShapeDtypeStruct((2, columns), F32),
            jax.ShapeDtypeStruct((devices * 2, 128), F32),
        ],
        scratch_shapes=[
            pltpu.VMEM((rows, width), BF16),
            pltpu.VMEM(aero.shape, BF16),
            pltpu.VMEM(kept.shape, BF16),
            pltpu.VMEM((rows, 2 * columns), BF16),
            pltpu.VMEM((2 * tiles, fields * 32, 128), F32),
            pltpu.VMEM((levels + 1, 8, columns), F32),
            twice(levels, glw, 128),
            twice(levels + 1, glw, 128),
            twice(levels, gsw, 128),
            twice(levels, gsw, 128),
            twice(glw + gsw, 256),
            pltpu.VMEM((glw, 128), F32),
            pltpu.VMEM((gsw, 128), F32),
            pltpu.VMEM((gsw, 128), F32),
            pltpu.VMEM((gsw, 128), F32),
            pltpu.VMEM((levels + 1, 8, columns), F32),
            pltpu.VMEM((levels + 1, 8, columns), F32),
            pltpu.SemaphoreType.DMA((2 + tiles,)),
        ],
        compiler_params=pltpu.CompilerParams(vmem_limit_bytes=54 * MIB),
        cost_estimate=pl.CostEstimate(flops=250 * count, bytes_accessed=12 * MIB, transcendentals=4 * count),
        name="flux",
    )(recv, aero, kept, coefficients, weights, coszen, albedo, ground, sunlit)


def local_kernel(me_ref, map_ref, heat_ref, out_ref):
    columns = map_ref.shape[1]
    goal = lax.broadcasted_iota(jnp.int32, (columns, columns), 0) + me_ref[0] * columns
    stay = onehot(map_ref[...] == goal)
    high, low = halves(heat_ref[...])
    out_ref[...] = jnp.dot(high, stay, preferred_element_type=F32) + jnp.dot(
        low, stay, preferred_element_type=F32
    )


def unpack_kernel(local_ref, pick_ref, back_ref, out_ref):
    devices = back_ref.shape[0] // 2
    levels = local_ref.shape[0]
    total = local_ref[...]
    for pair in range(2):
        high, low = halves(back_ref[pl.ds(pair, devices, stride=2), :])
        for side in range(2):
            place = 2 * pair + side
            pick = pick_ref[place * devices : (place + 1) * devices, :]
            part = lax.dot_general(high, pick, TN, preferred_element_type=F32) + lax.dot_general(
                low, pick, TN, preferred_element_type=F32
            )
            total = total + part[side * levels : (side + 1) * levels]
    out_ref[...] = total


def shards(
    dyn_state,
    span_map,
    sunlit,
    coszen,
    albedo,
    ground_temp,
    aerosol,
    k_long,
    planck,
    k_short,
    solar_flux,
):
    fields, levels, columns = dyn_state.shape
    devices = lax.axis_size("gx") * lax.axis_size("gy")
    me = lax.axis_index(AXES).astype(jnp.int32).reshape(1)
    map_row = span_map.reshape(1, columns)
    swap = functools.partial(lax.all_to_all, axis_name=AXES, split_axis=0, concat_axis=0, tiled=True)

    outgoing, pick = pack(me, map_row, dyn_state, devices)
    width = outgoing.shape[1]
    recv = swap(outgoing.reshape(devices, 2 * CAP, width)).reshape(devices * 2 * CAP, width)
    aero, kept, coefficients, weights = base(
        me, map_row, dyn_state, aerosol, k_long, k_short, planck, solar_flux
    )
    row = lambda x: x.reshape(1, columns)
    heat, surface, back = flux(
        recv,
        aero,
        kept,
        coefficients,
        weights,
        row(coszen),
        row(albedo),
        row(ground_temp),
        row(sunlit),
        fields,
        planck.shape[0],
    )

    returned = swap(back.reshape(devices, 2, 128)).reshape(devices * 2, 128)
    whole = pl.BlockSpec(memory_space=pltpu.VMEM)
    local = pl.pallas_call(
        local_kernel,
        in_specs=[pl.BlockSpec(memory_space=pltpu.SMEM), whole, whole],
        out_specs=whole,
        out_shape=jax.ShapeDtypeStruct((levels, columns), F32),
        cost_estimate=pl.CostEstimate(
            flops=4 * levels * columns * columns, bytes_accessed=MIB, transcendentals=0
        ),
        compiler_params=pltpu.CompilerParams(vmem_limit_bytes=8 * MIB),
        name="local",
    )(me, map_row, heat)
    heating = pl.pallas_call(
        unpack_kernel,
        in_specs=[whole] * 3,
        out_specs=whole,
        out_shape=jax.ShapeDtypeStruct((levels, columns), F32),
        cost_estimate=pl.CostEstimate(
            flops=8 * levels * columns * columns, bytes_accessed=MIB, transcendentals=0
        ),
        compiler_params=pltpu.CompilerParams(vmem_limit_bytes=8 * MIB),
        name="unpack",
    )(local, pick, returned)
    return heating, surface


def solution(mesh):
    cols = P(AXES)
    in_specs = (
        P(None, None, AXES),
        cols,
        cols,
        cols,
        cols,
        cols,
        P(None, None, AXES),
        P(),
        P(),
        P(),
        P(),
    )
    out_specs = (P(None, AXES), P(None, AXES))
    return jax.shard_map(shards, mesh=mesh, in_specs=in_specs, out_specs=out_specs, check_vma=False)
```

```python
import functools

import jax
import jax.numpy as jnp
from jax import lax
from jax.experimental import pallas as pl
from jax.experimental.pallas import tpu as pltpu
from jax.sharding import PartitionSpec as P

AXES = ("gx", "gy")
DIFFUSE = 1.66
SCATTER = 0.3
SW_DEPTH = 2.0
LOG2E = 1.4426950408889634
CAP = 4
BF16 = jnp.bfloat16
F32 = jnp.float32
NT = (((1,), (1,)), ((), ()))
TN = (((0,), (0,)), ((), ()))
MIB = 1 << 20
HEAD, TAIL = 48, 64


def onehot(mask):
    return jnp.where(mask, 1.0, 0.0).astype(BF16)


def halves(x):
    high = x.astype(BF16)
    return high, (x - high.astype(F32)).astype(BF16)


def softplus2(u):
    return jnp.maximum(u, jnp.log2(1.0 + jnp.exp2(jnp.minimum(u, 126.0))))


def pack_kernel(me_ref, map_ref, dyn_ref, out_ref, pick_ref, place_ref, meta_ref):
    columns = map_ref.shape[1]
    rows = place_ref.shape[0]
    devices = rows // (2 * CAP)
    step = pl.program_id(0)
    last = pl.num_programs(0) - 1

    @pl.when(step == 0)
    def _():
        where_to = map_ref[...]
        target = where_to // columns
        slot = where_to % columns
        same = target == lax.broadcasted_iota(jnp.int32, (devices, columns), 0)
        earlier = onehot(
            lax.broadcasted_iota(jnp.int32, (columns, columns), 0)
            < lax.broadcasted_iota(jnp.int32, (columns, columns), 1)
        )
        before = jnp.dot(onehot(same), earlier, preferred_element_type=F32)
        rank = jnp.sum(jnp.where(same, before, 0.0), axis=0, keepdims=True).astype(jnp.int32)
        rank = jnp.where(target == me_ref[0], CAP, rank)
        for place in range(CAP):
            pick_ref[place * devices : (place + 1) * devices, :] = onehot(same & (rank == place))
        key = jnp.where(rank < CAP, (target * CAP + rank) * 2, 2 * rows)
        line = lax.broadcasted_iota(jnp.int32, (128, columns), 0)
        mark = slot + 1
        meta = jnp.where(line == 0, mark // 2, jnp.where(line == 1, mark % 2, 0)).astype(F32)
        for half in range(2):
            lanes = slice(half * columns, (half + 1) * columns)
            meta_ref[:, lanes] = meta.astype(BF16)
            for start in range(0, rows, 128):
                line = lax.broadcasted_iota(jnp.int32, (128, columns), 0) + start
                place_ref[start : start + 128, lanes] = onehot(line == key + half)

    @pl.when(step < last)
    def _():
        count = dyn_ref.shape[0] * 32
        both = [dyn_ref[:, half * 32 : half * 32 + 32, :].reshape(count, columns) for half in range(2)]
        out_ref[...] = lax.dot_general(
            place_ref[...], jnp.concatenate(both, axis=1), NT, preferred_element_type=F32
        ).astype(BF16)

    @pl.when(step == last)
    def _():
        out_ref[:, :128] = lax.dot_general(
            place_ref[...], meta_ref[...], NT, preferred_element_type=F32
        ).astype(BF16)


def pack(me, map_row, dyn_state, devices):
    fields, levels, columns = dyn_state.shape
    steps = 1
    rows = devices * CAP * 2
    return pl.pallas_call(
        pack_kernel,
        grid=(steps + 1,),
        in_specs=[
            pl.BlockSpec(memory_space=pltpu.SMEM),
            pl.BlockSpec((1, columns), lambda i: (0, 0)),
            pl.BlockSpec((fields, levels, columns), lambda i: (jnp.minimum(i, steps - 1), 0, 0)),
        ],
        out_specs=[
            pl.BlockSpec((rows, fields * 32), lambda i: (0, i)),
            pl.BlockSpec((devices * CAP, columns), lambda i: (0, 0)),
        ],
        out_shape=[
            jax.ShapeDtypeStruct((rows, fields * 32 + 128), BF16),
            jax.ShapeDtypeStruct((devices * CAP, columns), BF16),
        ],
        scratch_shapes=[
            pltpu.VMEM((rows, 2 * columns), BF16),
            pltpu.VMEM((128, 2 * columns), BF16),
        ],
        compiler_params=pltpu.CompilerParams(vmem_limit_bytes=56 * MIB),
        cost_estimate=pl.CostEstimate(
            flops=4 * fields * levels * columns * devices * CAP, bytes_accessed=6 * MIB, transcendentals=0
        ),
        name="pack",
    )(me, map_row, dyn_state)


def base_kernel(
    me_ref,
    map_ref,
    dyn_ref,
    aer_ref,
    long_ref,
    short_ref,
    planck_ref,
    solar_ref,
    aero_ref,
    kept_ref,
    k_ref,
    weight_ref,
    pick_ref,
    rows_ref,
    wide_ref,
):
    fields, depth, columns = dyn_ref.shape
    extra = aer_ref.shape[0]
    tiles = columns // 128
    glw, gsw = long_ref.shape[0], short_ref.shape[0]

    @pl.when(pl.program_id(0) == 0)
    def _():
        goal = lax.broadcasted_iota(jnp.int32, (columns, columns), 0) + me_ref[0] * columns
        pick_ref[...] = onehot(map_ref[...] == goal)
        wide_ref[...] = jnp.zeros(wide_ref.shape, F32)
        for coefficients, start in ((long_ref[...], 0), (short_ref[...], glw)):
            scaled = coefficients.astype(F32) * LOG2E
            rows = slice(start, start + coefficients.shape[0])
            for first, part in zip((0, HEAD + TAIL), halves(scaled)):
                part = part.astype(F32)
                wide_ref[rows, first : first + fields] = part[:, :fields]
                wide_ref[rows, first + HEAD : first + HEAD + extra] = part[:, fields:]
        k_ref[...] = wide_ref[...].astype(BF16)
        square = lax.broadcasted_iota(jnp.int32, (128, 128), 0) == lax.broadcasted_iota(
            jnp.int32, (128, 128), 1
        )
        for source, start in ((planck_ref[...], 0), (solar_ref[...], glw)):
            size = source.shape[1]
            picked = jnp.where(square[:size, :size], source, 0.0)
            weight_ref[start : start + size, :] = jnp.broadcast_to(
                jnp.sum(picked, axis=1, keepdims=True), (size, 128)
            )

    kept = lax.dot_general(
        dyn_ref[...].reshape(fields * depth, columns), pick_ref[...], NT, preferred_element_type=F32
    )
    kept_ref[0] = kept.astype(BF16).reshape(fields, depth, columns)
    more = aer_ref[...].reshape(extra * depth, columns).astype(F32)
    for tile in range(tiles):
        rows_ref[tile] = more[:, tile * 128 : tile * 128 + 128]
    for tile in range(tiles):
        for level in range(depth):
            aero = rows_ref[tile, pl.ds(level, extra, stride=depth), :]
            aero_ref[tile, level] = jnp.concatenate(
                [aero, jnp.zeros((TAIL - extra, 128), F32)], axis=0
            ).astype(BF16)


def base(me, map_row, dyn_state, aerosol, k_long, k_short, planck, solar):
    fields, levels, columns = dyn_state.shape
    extra = aerosol.shape[0]
    glw, gsw = k_long.shape[0], k_short.shape[0]
    depth = 16
    tiles = columns // 128
    fixed = lambda *shape: pl.BlockSpec(shape, lambda i: (0,) * len(shape))
    return pl.pallas_call(
        base_kernel,
        grid=(levels // depth,),
        in_specs=[
            pl.BlockSpec(memory_space=pltpu.SMEM),
            fixed(1, columns),
            pl.BlockSpec((fields, depth, columns), lambda i: (0, i, 0)),
            pl.BlockSpec((extra, depth, columns), lambda i: (0, i, 0)),
            fixed(*k_long.shape),
            fixed(*k_short.shape),
            fixed(1, glw),
            fixed(1, gsw),
        ],
        out_specs=[
            pl.BlockSpec((tiles, depth, TAIL, 128), lambda i: (0, i, 0, 0)),
            pl.BlockSpec((1, fields, depth, columns), lambda i: (i // 2, 0, i % 2, 0)),
            fixed(glw + gsw, 2 * (HEAD + TAIL)),
            fixed(glw + gsw, 128),
        ],
        out_shape=[
            jax.ShapeDtypeStruct((tiles, levels, TAIL, 128), BF16),
            jax.ShapeDtypeStruct((2, fields, levels // 2, columns), BF16),
            jax.ShapeDtypeStruct((glw + gsw, 2 * (HEAD + TAIL)), BF16),
            jax.ShapeDtypeStruct((glw + gsw, 128), F32),
        ],
        scratch_shapes=[
            pltpu.VMEM((columns, columns), BF16),
            pltpu.VMEM((tiles, extra * depth, 128), F32),
            pltpu.VMEM((glw + gsw, 2 * (HEAD + TAIL)), F32),
        ],
        compiler_params=pltpu.CompilerParams(vmem_limit_bytes=62 * MIB),
        cost_estimate=pl.CostEstimate(
            flops=2 * fields * levels * columns * columns, bytes_accessed=14 * MIB, transcendentals=0
        ),
        name="base",
    )(me, map_row, dyn_state, aerosol, k_long, k_short, planck.reshape(1, glw), solar.reshape(1, gsw))


def flux_kernel(
    recv_hbm,
    aero_hbm,
    kept_hbm,
    k_ref,
    weight_ref,
    cos_ref,
    albedo_ref,
    ground_ref,
    lit_ref,
    heat_ref,
    surface_ref,
    back_ref,
    recv_ref,
    aero_ref,
    kept_ref,
    pick_ref,
    state_ref,
    delta_ref,
    trans_refs,
    down_refs,
    scat_refs,
    diff_refs,
    depth_refs,
    up_ref,
    beam_ref,
    spread_ref,
    return_ref,
    net_lw_ref,
    net_sw_ref,
    sems,
):
    rows = recv_ref.shape[0]
    devices = rows // (2 * CAP)
    tiles, levels, _, _ = aero_ref.shape
    columns = 128 * tiles
    glw, gsw = up_ref.shape[0], return_ref.shape[0]
    tall = state_ref.shape[1]
    fields = tall // 32
    pairs = levels // 2

    copies = [
        pltpu.make_async_copy(source, target, sems.at[i])
        for i, (source, target) in enumerate(
            [(recv_hbm, recv_ref), (kept_hbm, kept_ref)]
            + [(aero_hbm.at[tile], aero_ref.at[tile]) for tile in range(tiles)]
        )
    ]
    for copy in copies:
        copy.start()

    lanes_of = lambda tile: slice(tile * 128, tile * 128 + 128)
    copies[0].wait()
    mark = recv_ref[:, tall : tall + 128].astype(F32)
    mark = (mark[:, 0:1] * 2.0 + mark[:, 1:2]).astype(jnp.int32)
    half_of = lax.broadcasted_iota(jnp.int32, (rows, 1), 0) % 2
    for half in range(2):
        key = jnp.where(half_of == half, mark, 0)
        for tile in range(0, columns, 128):
            lane = lax.broadcasted_iota(jnp.int32, (rows, 128), 1) + (tile + 1)
            pick_ref[:, half * columns + tile : half * columns + tile + 128] = onehot(key == lane)
    copies[1].wait()
    for tile in range(0, tall, 128):
        moved = lax.dot_general(
            recv_ref[:, tile : tile + 128], pick_ref[...], TN, preferred_element_type=F32
        )
        for part in range(2 * tiles):
            stayed = kept_ref[part // tiles, tile // 32 : tile // 32 + 4, :, lanes_of(part % tiles)]
            state_ref[part, tile : tile + 128, :] = moved[:, lanes_of(part)] + stayed.reshape(
                128, 128
            ).astype(F32)

    for tile in range(tiles):
        cold = jnp.concatenate([state_ref[tile, :32, :], state_ref[tiles + tile, :32, :]], axis=0)
        warmth = softplus2(cold * LOG2E) * (1.0 / LOG2E)
        step = warmth - jnp.concatenate([warmth[1:], jnp.zeros((1, 128), F32)], axis=0)
        delta_ref[0, :, lanes_of(tile)] = jnp.broadcast_to(warmth[0:1], (8, 128))
        for level in range(levels):
            delta_ref[level + 1, :, lanes_of(tile)] = jnp.broadcast_to(step[level : level + 1], (8, 128))

    cosine, albedo, ground = cos_ref[...], albedo_ref[...], ground_ref[...]
    lit = lit_ref[...].astype(F32)
    slant = (-SW_DEPTH / levels) / cosine
    skin = softplus2(ground * LOG2E) * (1.0 / LOG2E)

    def absorb(pair, tile):
        half = pair // (pairs // 2)
        inner = 2 * pair - 32 * half
        both = [
            state_ref[half * tiles + tile, pl.ds(inner + e, fields, stride=32), :] for e in range(2)
        ]
        here = jnp.concatenate(
            [jnp.concatenate(both, axis=1), jnp.zeros((HEAD - fields, 256), F32)], axis=0
        ).astype(BF16)
        rest = jnp.concatenate([aero_ref[tile, 2 * pair + e] for e in range(2)], axis=1)
        return jnp.dot(
            k_ref[...], jnp.concatenate([here, rest, here, rest], axis=0), preferred_element_type=F32
        )

    def both_ways(pair, tile, depth_ref, following, following_tile, following_ref):
        descends, ascends = tile < tiles, tile > 0
        if descends:
            following_ref[...] = absorb(following, following_tile)
            trans_ref, down_ref = trans_refs[tile % 2], down_refs[tile % 2]
            scat_ref, diff_ref = scat_refs[tile % 2], diff_refs[tile % 2]
            level = 2 * pair
            lanes = lanes_of(tile)
            delta = [delta_ref[level + e + 1, :, lanes] for e in range(2)]
            slope = jnp.broadcast_to(slant[:, lanes], (8, 128))
            sum_beam = [jnp.zeros((8, 128), F32) for _ in range(2)]
            sum_spread = [jnp.zeros((8, 128), F32) for _ in range(2)]
        if ascends:
            old_trans, old_down = trans_refs[1 - tile % 2], down_refs[1 - tile % 2]
            old_scat, old_diff = scat_refs[1 - tile % 2], diff_refs[1 - tile % 2]
            old_level = 2 * (pairs - 1 - pair)
            old_lanes = lanes_of(tile - 1)
            old_delta = [delta_ref[old_level + e, :, old_lanes] for e in range(2)]
            total_lw = [jnp.zeros((8, 128), F32) for _ in range(2)]
            total_sw = [net_sw_ref[old_level + e, :, old_lanes] for e in range(2)]

        for g in range(0, glw, 8):
            if descends:
                down = down_ref[level, g : g + 8, :]
                for e in range(2):
                    u = depth_ref[g : g + 8, 128 * e : 128 * e + 128]
                    tau = jnp.log2(1.0 + jnp.exp2(jnp.minimum(u, 126.0)))
                    trans = jnp.exp2(tau * (-DIFFUSE))
                    trans_ref[level + e, g : g + 8, :] = trans
                    down = trans * down + delta[e]
                    down_ref[level + e + 1, g : g + 8, :] = down
            if ascends:
                upper = up_ref[g : g + 8, :]
                weight = weight_ref[g : g + 8, :]
                for e in (1, 0):
                    passed = old_trans[old_level + e, g : g + 8, :] * upper
                    total_lw[e] = total_lw[e] + weight * (old_down[old_level + e, g : g + 8, :] - passed)
                    upper = passed - old_delta[e]
                up_ref[g : g + 8, :] = upper
        for g in range(0, gsw, 8):
            if descends:
                beam = beam_ref[g : g + 8, :]
                spread = spread_ref[g : g + 8, :]
                for e in range(2):
                    u = depth_ref[glw + g : glw + g + 8, 128 * e : 128 * e + 128]
                    tau = jnp.maximum(u, jnp.log2(1.0 + jnp.exp2(jnp.minimum(u, 126.0))))
                    diffuse = jnp.exp2(tau * (-DIFFUSE * SW_DEPTH / levels))
                    diff_ref[level + e, g : g + 8, :] = diffuse
                    lower = jnp.exp2(tau * slope) * beam
                    scattered = beam - lower
                    scat_ref[level + e, g : g + 8, :] = scattered
                    sum_beam[e] = sum_beam[e] + beam
                    sum_spread[e] = sum_spread[e] + spread
                    spread = diffuse * spread + scattered
                    beam = lower
                beam_ref[g : g + 8, :] = beam
                spread_ref[g : g + 8, :] = spread
            if ascends:
                upper = return_ref[g : g + 8, :]
                for e in (1, 0):
                    upper = (
                        old_diff[old_level + e, g : g + 8, :] * upper
                        + old_scat[old_level + e, g : g + 8, :]
                    )
                    total_sw[e] = total_sw[e] - upper
                return_ref[g : g + 8, :] = upper
        for e in range(2):
            if descends:
                net_sw_ref[level + e, :, lanes] = sum_beam[e] * (1.0 / SCATTER) + sum_spread[e]
            if ascends:
                net_lw_ref[old_level + e, :, old_lanes] = total_lw[e]
                net_sw_ref[old_level + e, :, old_lanes] = total_sw[e]

    def turn(tile):
        lanes = lanes_of(tile)
        down_ref = down_refs[tile % 2]
        total = jnp.zeros((8, 128), F32)
        floor_total = jnp.zeros((8, 128), F32)
        upper = jnp.broadcast_to(skin[:, lanes], (8, 128))
        above = upper - delta_ref[levels, :, lanes]
        for g in range(0, glw, 8):
            weight = weight_ref[g : g + 8, :]
            floor = weight * down_ref[levels, g : g + 8, :]
            floor_total = floor_total + floor
            total = total + (floor - weight * upper)
            up_ref[g : g + 8, :] = above
        net_lw_ref[levels, :, lanes] = total
        surface_ref[0:1, lanes] = jnp.sum(floor_total, axis=0, keepdims=True) * (1.0 / glw)
        bright = jnp.broadcast_to(albedo[:, lanes], (8, 128))
        floor_total = jnp.zeros((8, 128), F32)
        for g in range(0, gsw, 8):
            floor = beam_ref[g : g + 8, :] * (1.0 / SCATTER) + spread_ref[g : g + 8, :]
            floor_total = floor_total + floor
            return_ref[g : g + 8, :] = bright * floor
        net_sw_ref[levels, :, lanes] = floor_total - bright * floor_total
        surface_ref[1:2, lanes] = jnp.sum(floor_total, axis=0, keepdims=True) * (
            lit[:, lanes] * cosine[:, lanes] * (1.0 / gsw)
        )

    copies[2].wait()
    depth_refs[0][...] = absorb(0, 0)
    for tile in range(tiles + 1):
        if tile + 1 < tiles:
            copies[2 + tile + 1].wait()
        if tile < tiles:
            first = 0.0 - delta_ref[0, :, lanes_of(tile)]
            for g in range(0, glw, 8):
                down_refs[tile % 2][0, g : g + 8, :] = first
            spread_ref[...] = jnp.zeros((gsw, 128), F32)
            beam_ref[...] = SCATTER * weight_ref[glw:, :]

        def two_pairs(step, _, tile=tile):
            for part in range(2):
                pair = 2 * step + part
                over = pair == pairs - 1
                following = jnp.where(over, 0, pair + 1)
                following_tile = jnp.where(over, min(tile + 1, tiles - 1), tile)
                both_ways(
                    pair, tile, depth_refs[part], following, following_tile, depth_refs[1 - part]
                )
            return 0

        lax.fori_loop(0, pairs // 2, two_pairs, 0, unroll=8)
        if tile < tiles:
            turn(tile)

    net_lw = jnp.sum(net_lw_ref[...], axis=1)
    net_sw = jnp.sum(net_sw_ref[...], axis=1)
    heat = (net_lw[:levels] - net_lw[1 : levels + 1]) * (1.0 / glw) + (
        net_sw[:levels] - net_sw[1 : levels + 1]
    ) * (lit * cosine * (1.0 / gsw))
    heat_ref[...] = heat

    twice = jnp.concatenate([heat, heat], axis=0)
    high, low = halves(twice)
    picked = pick_ref[:, :columns]
    state_ref[0, :rows, :] = lax.dot_general(picked, high, NT, preferred_element_type=F32) + lax.dot_general(
        picked, low, NT, preferred_element_type=F32
    )
    left = lax.broadcasted_iota(jnp.int32, (devices, 128), 1) < levels
    for pair in range(2):
        even = state_ref[0, pl.ds(4 * pair, devices, stride=8), :]
        odd = state_ref[0, pl.ds(4 * pair + 2, devices, stride=8), :]
        back_ref[pl.ds(pair, devices, stride=2), :] = jnp.where(left, even, odd)


def flux(recv, aero, kept, coefficients, weights, coszen, albedo, ground, sunlit, fields, glw):
    rows, width = recv.shape
    tiles, levels, _, _ = aero.shape
    columns = 128 * tiles
    gsw = weights.shape[0] - glw
    devices = rows // (2 * CAP)
    whole = pl.BlockSpec(memory_space=pltpu.VMEM)
    count = (glw + gsw) * levels * columns
    twice = lambda *shape: [pltpu.VMEM(shape, F32)] * 2
    return pl.pallas_call(
        flux_kernel,
        in_specs=[pl.BlockSpec(memory_space=pl.ANY)] * 3 + [whole] * 6,
        out_specs=[whole] * 3,
        out_shape=[
            jax.ShapeDtypeStruct((levels, columns), F32),
            jax.ShapeDtypeStruct((2, columns), F32),
            jax.ShapeDtypeStruct((devices * 2, 128), F32),
        ],
        scratch_shapes=[
            pltpu.VMEM((rows, width), BF16),
            pltpu.VMEM(aero.shape, BF16),
            pltpu.VMEM(kept.shape, BF16),
            pltpu.VMEM((rows, 2 * columns), BF16),
            pltpu.VMEM((2 * tiles, fields * 32, 128), F32),
            pltpu.VMEM((levels + 1, 8, columns), F32),
            twice(levels, glw, 128),
            twice(levels + 1, glw, 128),
            twice(levels, gsw, 128),
            twice(levels, gsw, 128),
            twice(glw + gsw, 256),
            pltpu.VMEM((glw, 128), F32),
            pltpu.VMEM((gsw, 128), F32),
            pltpu.VMEM((gsw, 128), F32),
            pltpu.VMEM((gsw, 128), F32),
            pltpu.VMEM((levels + 1, 8, columns), F32),
            pltpu.VMEM((levels + 1, 8, columns), F32),
            pltpu.SemaphoreType.DMA((2 + tiles,)),
        ],
        compiler_params=pltpu.CompilerParams(vmem_limit_bytes=54 * MIB),
        cost_estimate=pl.CostEstimate(flops=250 * count, bytes_accessed=12 * MIB, transcendentals=4 * count),
        name="flux",
    )(recv, aero, kept, coefficients, weights, coszen, albedo, ground, sunlit)


def local_kernel(me_ref, map_ref, heat_ref, out_ref):
    columns = map_ref.shape[1]
    goal = lax.broadcasted_iota(jnp.int32, (columns, columns), 0) + me_ref[0] * columns
    stay = onehot(map_ref[...] == goal)
    high, low = halves(heat_ref[...])
    out_ref[...] = jnp.dot(high, stay, preferred_element_type=F32) + jnp.dot(
        low, stay, preferred_element_type=F32
    )


def unpack_kernel(local_ref, pick_ref, back_ref, out_ref):
    devices = back_ref.shape[0] // 2
    levels = local_ref.shape[0]
    total = local_ref[...]
    for pair in range(2):
        high, low = halves(back_ref[pl.ds(pair, devices, stride=2), :])
        for side in range(2):
            place = 2 * pair + side
            pick = pick_ref[place * devices : (place + 1) * devices, :]
            part = lax.dot_general(high, pick, TN, preferred_element_type=F32) + lax.dot_general(
                low, pick, TN, preferred_element_type=F32
            )
            total = total + part[side * levels : (side + 1) * levels]
    out_ref[...] = total


def shards(
    dyn_state,
    span_map,
    sunlit,
    coszen,
    albedo,
    ground_temp,
    aerosol,
    k_long,
    planck,
    k_short,
    solar_flux,
):
    fields, levels, columns = dyn_state.shape
    devices = lax.axis_size("gx") * lax.axis_size("gy")
    me = lax.axis_index(AXES).astype(jnp.int32).reshape(1)
    map_row = span_map.reshape(1, columns)
    swap = functools.partial(lax.all_to_all, axis_name=AXES, split_axis=0, concat_axis=0, tiled=True)

    outgoing, pick = pack(me, map_row, dyn_state, devices)
    width = outgoing.shape[1]
    recv = swap(outgoing.reshape(devices, 2 * CAP, width)).reshape(devices * 2 * CAP, width)
    aero, kept, coefficients, weights = base(
        me, map_row, dyn_state, aerosol, k_long, k_short, planck, solar_flux
    )
    row = lambda x: x.reshape(1, columns)
    heat, surface, back = flux(
        recv,
        aero,
        kept,
        coefficients,
        weights,
        row(coszen),
        row(albedo),
        row(ground_temp),
        row(sunlit),
        fields,
        planck.shape[0],
    )

    returned = swap(back.reshape(devices, 2, 128)).reshape(devices * 2, 128)
    whole = pl.BlockSpec(memory_space=pltpu.VMEM)
    local = pl.pallas_call(
        local_kernel,
        in_specs=[pl.BlockSpec(memory_space=pltpu.SMEM), whole, whole],
        out_specs=whole,
        out_shape=jax.ShapeDtypeStruct((levels, columns), F32),
        cost_estimate=pl.CostEstimate(
            flops=4 * levels * columns * columns, bytes_accessed=MIB, transcendentals=0
        ),
        compiler_params=pltpu.CompilerParams(vmem_limit_bytes=8 * MIB),
        name="local",
    )(me, map_row, heat)
    heating = pl.pallas_call(
        unpack_kernel,
        in_specs=[whole] * 3,
        out_specs=whole,
        out_shape=jax.ShapeDtypeStruct((levels, columns), F32),
        cost_estimate=pl.CostEstimate(
            flops=8 * levels * columns * columns, bytes_accessed=MIB, transcendentals=0
        ),
        compiler_params=pltpu.CompilerParams(vmem_limit_bytes=8 * MIB),
        name="unpack",
    )(local, pick, returned)
    return heating, surface


def solution(mesh):
    cols = P(AXES)
    in_specs = (
        P(None, None, AXES),
        cols,
        cols,
        cols,
        cols,
        cols,
        P(None, None, AXES),
        P(),
        P(),
        P(),
        P(),
    )
    out_specs = (P(None, AXES), P(None, AXES))
    return jax.shard_map(shards, mesh=mesh, in_specs=in_specs, out_specs=out_specs, check_vma=False)
```
